128 devices in a mesh: grp: 4 (over y), tile: 32 (over x, z, core).
Axes of the slice: x: 4, y: 4, z: 4, core: 2. Of those that a mesh axis runs over, the one named last changes fastest.
Arguments:
- inverse_factor: bfloat16 [128, 2560, 2560], P(('grp', 'tile')), as said below
- border: bfloat16 [128, 2560, 512], P(('grp', 'tile')), as said below
- border_blocks: int32 [128, 4], P(('grp', 'tile')), may hold values from 0 to 31, as said below
- border_count: int32 [128], P(('grp', 'tile')), may hold values from 1 to 4, as said below
- first_diag: float32 [4096], P('tile'), may hold values from 0.5 to 2
Outputs:
- panel: float32 [4096, 256], P('tile')
- reduced: float32 [4096, 4096], P('tile')
The draws below stay inside these ranges and needn't reach their ends.
Inputs may be any that keep to these rules, and one draw needn't show every extreme that they name: `border_blocks`: the entries of a row are distinct first-section block numbers; only the first border_count entries of a row are live. `border_count`: some scenario has 4 live blocks and some has 1. `inverse_factor`: each matrix is lower triangular with a diagonal between 1 and 2. `border`: real entries, most of magnitude below 3 / sqrt(20480).
All inputs are finite; a program needn't handle non-finite values.
Results may differ from the reference program's by a relative error of at most 0.0003.
Values sent between devices are 32-bit elements; how exact they have to be, the bound alone decides.
A program may use at most 192 MiB of HBM per device.

```python
import jax
import jax.numpy as jnp
from jax import lax

ORDER = 2560
FIRST = 4096
BLK = 128
MAXB = 4
PANELS = 2
SCEN = 128
MB = 512


def draw_inverse_factor(key, part):
    key = jax.random.fold_in(key, 11)
    rowi = lax.broadcasted_iota(jnp.int32, (ORDER, ORDER), 0)
    coli = lax.broadcasted_iota(jnp.int32, (ORDER, ORDER), 1)

    def one_matrix(index):
        sub = jax.random.fold_in(key, index)
        first_key, second_key = jax.random.split(sub, 2)
        diagonal = jax.random.uniform(first_key, (ORDER, 1), jnp.float32, 1.0, 2.0)
        spread = jax.random.normal(second_key, (ORDER, ORDER), jnp.float32)
        matrix = jnp.where(coli < rowi, spread * ORDER ** (-0.5), 0.0) + jnp.where(coli == rowi, diagonal, 0.0)
        return matrix.astype(jnp.bfloat16)
    return lax.map(one_matrix, jnp.arange(SCEN))


def draw_border(key, part):
    key = jax.random.fold_in(key, 53)
    factor = (56.0 * ORDER) ** (-0.5)

    def one_border(index):
        sub = jax.random.fold_in(key, index)
        first_key, second_key, third_key = jax.random.split(sub, 3)
        along = jnp.clip(jax.random.normal(first_key, (ORDER, 1), jnp.float32), -4.0, 4.0)
        weights = jnp.clip(jax.random.normal(second_key, (1, MB), jnp.float32), -4.0, 4.0)
        noise = jnp.clip(jax.random.normal(third_key, (ORDER, MB), jnp.float32), -4.0, 4.0)
        values = (along * weights * 1.4142135 + noise) * factor
        return values.astype(jnp.bfloat16)
    return lax.map(one_border, jnp.arange(SCEN))


def draw_border_blocks(key, part):
    key = jax.random.fold_in(key, 37)
    nblk = FIRST // BLK
    first_key, second_key = jax.random.split(key)
    scores = jax.random.randint(first_key, (SCEN, nblk), 0, 2 ** 20) * nblk + jnp.arange(nblk)[None, :]
    chosen = jax.random.randint(second_key, (), 0, SCEN)
    rows = lax.broadcasted_iota(jnp.int32, (SCEN, nblk), 0)
    cols = lax.broadcasted_iota(jnp.int32, (SCEN, nblk), 1)
    forced = (rows == chosen) & ((cols == 0) | (cols == nblk - 1))
    scores = jnp.where(forced, -1 - cols, scores)
    ordering = jnp.argsort(scores, axis=1)
    return ordering[:, :MAXB].astype(jnp.int32)


def draw_border_count(key, part):
    key = jax.random.fold_in(key, 23)
    first_key, second_key, third_key = jax.random.split(key, 3)
    drawn = jax.random.randint(first_key, (SCEN,), 1, MAXB + 1)
    biggest = jax.random.randint(second_key, (), 0, SCEN)
    smallest = (biggest + 1 + jax.random.randint(third_key, (), 0, SCEN - 1)) % SCEN
    index = jnp.arange(SCEN)
    return jnp.where(index == biggest, MAXB, jnp.where(index == smallest, 1, drawn)).astype(jnp.int32)


def shard_levels(stream_key, extent, cuts, low, largest):
    level, own = 1.0, jax.random.fold_in(stream_key, 6)
    for position, parts in cuts:
        draws = jnp.exp(jax.random.uniform(jax.random.fold_in(own, position), (parts,), jnp.float32, low / len(cuts), largest / len(cuts)))
        level = level * jnp.repeat(draws, extent[position] // parts).reshape([-1 if axis == position else 1 for axis in range(len(extent))])
    return level


def setup_inputs(seed: int = 0) -> dict:
    streams_of = jax.random.split(jax.random.key(seed), 6)
    inverse_factor = draw_inverse_factor(jax.random.fold_in(streams_of[5], 71), 0)
    border = draw_border(jax.random.fold_in(streams_of[5], 71), 0)
    border_blocks = draw_border_blocks(jax.random.fold_in(streams_of[5], 71), 0)
    border_count = draw_border_count(jax.random.fold_in(streams_of[5], 71), 0)
    first_diag = jnp.clip(0.5 + 1.5 * jax.random.uniform(streams_of[4], (FIRST,), jnp.float32) ** shard_levels(streams_of[4], (FIRST,), ((0, 32),), -0.2, 0.2), 0.5, 2.0)
    return {"inverse_factor": inverse_factor, "border": border, "border_blocks": border_blocks, "border_count": border_count, "first_diag": first_diag}


def reference(inverse_factor, border, border_blocks, border_count, first_diag):
    width = MAXB * BLK

    def add_one(total, item):
        factor, coupling, blocks, count = item
        live = (jnp.arange(width) // BLK < count).astype(jnp.bfloat16)
        coupled = jnp.dot(factor.astype(jnp.float32), (coupling * live[None, :]).astype(jnp.float32), preferred_element_type=jnp.float32).astype(jnp.bfloat16)
        gram = jnp.dot(coupled.T.astype(jnp.float32), coupled.astype(jnp.float32), preferred_element_type=jnp.float32)
        where_cols = (blocks[:, None] * BLK + jnp.arange(BLK)[None, :]).reshape(-1).astype(jnp.int32)
        total = total.at[where_cols[:, None], where_cols[None, :]].add(gram)
        return (total, None)
    start = jnp.zeros((FIRST, FIRST), jnp.float32)
    schur, _ = lax.scan(add_one, start, (inverse_factor, border, border_blocks, border_count))
    schur = schur + jnp.diag(first_diag)
    glob = jnp.arange(FIRST)
    columns = []
    for step in range(PANELS):
        block = schur[step * BLK:(step + 1) * BLK, step * BLK:(step + 1) * BLK]
        lower = jnp.linalg.cholesky(block)
        column = lax.linalg.triangular_solve(lower, schur[:, step * BLK:(step + 1) * BLK], left_side=False, lower=True, transpose_a=True)
        column = jnp.where((glob >= step * BLK)[:, None], column, 0.0)
        schur = schur - jnp.dot(column, column.T, precision=lax.Precision.HIGHEST)
        columns.append(column)
    return (jnp.concatenate(columns, axis=1), schur)
```

```python
import functools

import jax
import jax.numpy as jnp
from jax import lax
from jax.experimental import pallas as pl
from jax.experimental.pallas import tpu as pltpu
from jax.sharding import PartitionSpec as P

BLK = 128
MAXB = 4
NBLK = 32
ORDER = 2560
WIDTH = MAXB * BLK
DEV = 128
GRP = 4
TILE = 32
QUART = NBLK // GRP
STRIP = 512
STRIPS = ORDER // STRIP
PIECE1 = 24
PIECE2 = 16
PLACED = DEV * MAXB * MAXB
DEPTH = PLACED + BLK
MESH = pl.DeviceIdType.MESH
F32 = jnp.float32
BF16 = jnp.bfloat16
HIGHEST = lax.Precision.HIGHEST


def split(value):
    high = value.astype(BF16)
    return high, (value - high.astype(F32)).astype(BF16)


def dot(left, right, dims=((1,), (0,))):
    return lax.dot_general(left, right, (dims, ((), ())), preferred_element_type=F32)


def dot3(left, right, dims=((1,), (0,))):
    return dot(left[0], right[0], dims) + (dot(left[0], right[1], dims) + dot(left[1], right[0], dims))


def iota(shape, axis):
    return lax.broadcasted_iota(jnp.int32, shape, axis)


def peer_of(k, g, t):
    x, z, c = t // 8, (t // 2) % 4, t % 2
    dy, dx, dz, dc = k // 32, (k // 8) % 4, (k // 2) % 4, k % 2
    return (g + dy) % 4, ((x + dx) % 4) * 8 + ((z + dz) % 4) * 2 + (c + dc) % 2


class Ring:
    def __init__(self, view, own, me, up, down, send, recv, first):
        self.view, self.own, self.me = view, own, me
        self.up, self.down = up, down
        self.send, self.recv, self.first = send, recv, first

    def copy(self, src, dst, slot, device):
        made = pltpu.make_async_remote_copy(
            src, dst, self.send.at[self.first + slot], self.recv.at[self.first + slot],
            device_id=device, device_id_type=MESH)
        made.start()
        return made

    def start(self):
        me = self.me
        self.copies = [
            self.copy(self.own(0), self.view(me, 0), 0, self.up),
            self.copy(self.own(1), self.view(me, 1), 1, self.down),
            self.copy(self.own(1), self.view(me, 1), 2, self.up),
            self.copy(self.own(0), self.view(me, 0), 3, self.down),
        ]

    def middle(self):
        below, above = (self.me + 3) % 4, (self.me + 1) % 4
        self.copies[0].wait_recv()
        self.copies.append(self.copy(self.view(below, 0), self.view(below, 0), 4, self.up))
        self.copies[1].wait_recv()
        self.copies.append(self.copy(self.view(above, 1), self.view(above, 1), 5, self.down))

    def end(self):
        for made in self.copies[2:]:
            made.wait_recv()
        for made in self.copies:
            made.wait_send()


def factor_steps(a_ref, v_ref, first, last):
    sub = iota((8, BLK), 0)
    lane = iota((8, BLK), 1)

    def step(s, carry):
        base = pl.multiple_of(s * 8, 8)
        rows = a_ref[pl.ds(base, 8), :]
        inv_rows = v_ref[pl.ds(base, 8), :]
        cols = [
            jnp.take_along_axis(rows, jnp.full((8, BLK), base + p, jnp.int32), axis=1) for p in range(8)
        ]
        scale = jnp.zeros((8, BLK), F32)
        for p in range(8):
            recip = 1.0 / cols[p][p:p + 1, :]
            scale = jnp.where(sub == p, recip, scale)
            if p == 7:
                break
            by = jnp.where(sub > p, cols[p] * recip, 0.0)
            rows = rows - by * rows[p:p + 1, :]
            inv_rows = inv_rows - by * inv_rows[p:p + 1, :]
            for q in range(p + 1, 8):
                cols[q] = cols[q] - by * cols[q][p:p + 1, :]
        by = jnp.where(lane >= base + 8, rows * scale, 0.0).T
        a = a_ref[...]
        v = v_ref[...]
        for p in range(8):
            column = jnp.broadcast_to(by[:, p:p + 1], (BLK, BLK))
            a = a - column * rows[p:p + 1, :]
            v = v - column * inv_rows[p:p + 1, :]
        a_ref[...] = a
        v_ref[...] = v
        v_ref[pl.ds(base, 8), :] = inv_rows * jnp.sqrt(scale)
        return carry

    lax.fori_loop(first, last, step, 0)


def kernel(
    w_ref, b_ref, diag_ref, ids_ref, count_ref, panel_ref, reduced_ref,
    wbuf, bbuf, gram, send1, recv1, rhs, schur, send2, recv2, rows_all, cross, pivot, inverse,
    wsem, bsem, send_sem, recv_sem, own_sem, ring_send, ring_recv, core_send, core_recv,
):
    g = lax.axis_index("grp")
    t = lax.axis_index("tile")
    me = g * TILE + t
    x, z, c = t // 8, (t // 2) % 4, t % 2

    loads = []
    for i in range(STRIPS):
        rows = pl.ds(i * STRIP, STRIP)
        border = pltpu.make_async_copy(b_ref.at[0, rows], bbuf.at[rows], bsem.at[i])
        border.start()
        cols = pl.ds(0, (i + 1) * STRIP)
        factor = pltpu.make_async_copy(w_ref.at[0, rows, cols], wbuf.at[rows, cols], wsem.at[i])
        factor.start()
        loads.append((border, factor))

    barrier = pltpu.get_barrier_semaphore()

    def greet(k, carry):
        pl.semaphore_signal(barrier, inc=1, device_id=peer_of(k, g, t), device_id_type=MESH)
        return carry

    lax.fori_loop(1, DEV, greet, 0)

    live = iota((STRIP, WIDTH), 1) // BLK < count_ref[0]
    for i in range(STRIPS):
        rows = pl.ds(i * STRIP, STRIP)
        depth = pl.ds(0, (i + 1) * STRIP)
        loads[i][0].wait()
        bbuf[rows, :] = jnp.where(live, bbuf[rows, :], BF16(0))
        loads[i][1].wait()
        coupled = dot(wbuf[rows, depth], bbuf[depth, :]).astype(BF16)
        part = dot(coupled, coupled, ((0,), (0,)))
        if i == 0:
            gram[...] = part
        else:
            gram[...] += part

    for i in range(MAXB):
        for j in range(MAXB):
            send1[:, i * MAXB + j, :] = gram[i * BLK:(i + 1) * BLK, j * BLK:(j + 1) * BLK]
    lane = iota((BLK, BLK), 1)
    extra = jnp.where(lane == MAXB, jnp.broadcast_to(diag_ref[...], (BLK, BLK)).T, 0.0)
    for i in range(MAXB):
        extra = jnp.where(lane == i, ids_ref[0, i].astype(F32), extra)
    send1[:, MAXB * MAXB, :] = extra
    for i in range(MAXB * MAXB + 1, PIECE1):
        send1[:, i, :] = jnp.zeros((BLK, BLK), F32)

    pl.semaphore_wait(barrier, DEV - 1)

    def exchange(source, target, slot):
        def go(k, carry):
            g2, t2 = peer_of(k, g, t)
            pltpu.make_async_remote_copy(
                source.at[g2 * TILE + t2], target.at[me], send_sem.at[slot], recv_sem.at[slot],
                device_id=(g2, t2), device_id_type=MESH).start()
            return carry

        lax.fori_loop(1, DEV, go, 0)
        own = pltpu.make_async_copy(source.at[me], target.at[me], own_sem.at[slot])
        own.start()
        own.wait()
        every = pltpu.make_async_remote_copy(
            source.at[pl.ds(0, DEV - 1)], target.at[pl.ds(0, DEV - 1)], send_sem.at[slot],
            recv_sem.at[slot], device_id=(g, t), device_id_type=MESH)
        every.wait_recv()
        return every

    sent1 = exchange(send1, recv1, 0)

    extras = recv1[:, MAXB * MAXB, :]
    sel = iota((BLK, BLK), 0)
    pos = lane % (MAXB * MAXB)
    ids16 = extras.astype(BF16)
    at_lane = (sel % 8 == lane // (MAXB * MAXB)).astype(F32)
    gather = (iota((DEV // 8, DEV), 1) // 8 == iota((DEV // 8, DEV), 0)).astype(BF16)

    def along(which):
        spread = dot(ids16, (sel == which).astype(BF16)) * at_lane
        return dot(gather, spread.astype(BF16))

    keys = (along(pos // MAXB) * NBLK + along(pos % MAXB)).astype(jnp.int32)
    own_row = iota((1, BLK), 1)
    own_key = jnp.where(own_row < NBLK, own_row * (NBLK + 1), -1)
    diag = jnp.where((lane == me) & (sel < NBLK), jnp.broadcast_to(extras[:, MAXB:MAXB + 1], (BLK, BLK)), 0.0)
    high, low = split(recv1[:, 0:MAXB * MAXB, :].reshape(PLACED, BLK))
    rhs[0:PLACED, 0:BLK] = high
    rhs[0:PLACED, BLK:2 * BLK] = low
    high, low = split(diag)
    rhs[PLACED:DEPTH, 0:BLK] = high
    rhs[PLACED:DEPTH, BLK:2 * BLK] = low

    def place(m, carry):
        base = pl.multiple_of(m * 256, 256)
        target = iota((256, BLK), 0) + base
        hot = [
            jnp.where(target == keys[q:q + 1, :], F32(1), F32(0)).astype(BF16) for q in range(DEV // 8)
        ]
        hot.append(jnp.where(target == own_key, F32(1), F32(0)).astype(BF16))
        both = dot(jnp.concatenate(hot, axis=1), rhs[...])
        schur[pl.ds(base, 256), :] = both[:, 0:BLK] + both[:, BLK:2 * BLK]
        return carry

    lax.fori_loop(0, NBLK * NBLK // 256, place, 0)

    for h in range(GRP):
        for u in range(TILE):
            send2[h * TILE + u, 0:QUART, :] = schur[u * NBLK + h * QUART:u * NBLK + (h + 1) * QUART, :]
        some = pl.ds(h * TILE, TILE)
        for b in range(2):
            send2[some, QUART + b, :] = schur[b * NBLK:(b + 1) * NBLK, :]
            for e in range(2):
                send2[some, QUART + 2 + 2 * b + e, :] = jnp.broadcast_to(
                    schur[b * NBLK + e:b * NBLK + e + 1, :], (TILE, BLK))
            send2[some, QUART + 6 + b, :] = jnp.zeros((TILE, BLK), F32)
    sent2 = exchange(send2, recv2, 1)

    quarter = pltpu.make_async_copy(recv2.at[:, pl.ds(0, QUART)], rows_all.at[g], own_sem.at[2])
    quarter.start()
    for b in range(2):
        cross[b, x, z, c] = recv2[:, QUART + b, :]

    half = BLK // 2
    side = lambda s: pl.ds(s * half, half)
    at_x = lambda i: (g, i * 8 + z * 2 + c)
    at_z = lambda i: (g, x * 8 + i * 2 + c)
    up, down = (lambda i: (i + 1) % 4), (lambda i: (i + 3) % 4)
    ring_y = Ring(
        lambda i, s: rows_all.at[i, side(s)], lambda s: recv2.at[side(s), pl.ds(0, QUART)], g,
        (up(g), t), (down(g), t), ring_send, ring_recv, 0)

    def ring(view, position, at, first):
        return Ring(view, lambda s: view(position, s), position, at(up(position)), at(down(position)),
                    ring_send, ring_recv, first)

    ring_a1 = ring(lambda i, s: cross.at[0, i, z, c, side(s)], x, at_x, 6)
    ring_b1 = ring(lambda i, s: cross.at[1, x, i, c, side(s)], z, at_z, 12)
    ring_a2 = ring(lambda i, s: cross.at[0, :, i, c, side(s)], z, at_z, 18)
    ring_b2 = ring(lambda i, s: cross.at[1, i, :, c, side(s)], x, at_x, 24)

    ring_y.start()
    ring_a1.start()
    ring_b1.start()

    eye = jnp.where(sel == lane, F32(1), F32(0))
    pivot[...] = recv2[:, QUART + 2, :]
    inverse[0] = eye
    inverse[1] = eye
    factor_steps(pivot, inverse.at[0], 0, 4)
    ring_a1.middle()
    ring_b1.middle()
    factor_steps(pivot, inverse.at[0], 4, 8)
    ring_y.middle()
    ring_a1.end()
    ring_b1.end()
    ring_a2.start()
    ring_b2.start()
    factor_steps(pivot, inverse.at[0], 8, 16)
    ring_a2.middle()
    ring_b2.middle()
    below = lax.dot_general(
        recv2[:, QUART + 4, :], inverse[0], (((1,), (1,)), ((), ())), precision=HIGHEST,
        preferred_element_type=F32)
    pivot[...] = recv2[:, QUART + 5, :] - lax.dot_general(
        below, below, (((1,), (1,)), ((), ())), precision=HIGHEST, preferred_element_type=F32)
    factor_steps(pivot, inverse.at[1], 0, 8)
    ring_a2.end()
    ring_b2.end()
    other = (g, x * 8 + z * 2 + (1 - c))
    swaps = [
        pltpu.make_async_remote_copy(
            cross.at[b, :, :, c], cross.at[b, :, :, c], core_send.at[b], core_recv.at[b],
            device_id=other, device_id_type=MESH) for b in range(2)
    ]
    for swap in swaps:
        swap.start()
    factor_steps(pivot, inverse.at[1], 8, 16)
    first, second = inverse[0], inverse[1]
    mixed = -jnp.dot(
        second, jnp.dot(below, first, precision=HIGHEST, preferred_element_type=F32),
        precision=HIGHEST, preferred_element_type=F32)
    inv = split(jnp.concatenate(
        [jnp.concatenate([first, jnp.zeros((BLK, BLK), F32)], axis=1),
         jnp.concatenate([mixed, second], axis=1)], axis=0))

    quarter.wait()
    ring_y.end()
    own_cols = split(jnp.concatenate([rows_all[0, :, 0, :], rows_all[0, :, 1, :]], axis=1))
    panel = dot3(own_cols, inv, ((1,), (1,)))
    panel = jnp.where((t == 0) & (iota((BLK, 2 * BLK), 1) >= BLK), 0.0, panel)
    panel_ref[...] = panel
    panel = split(panel)
    for swap in swaps:
        swap.wait_recv()

    def update(n, carry):
        x2, z2 = n // 4, n % 4
        column = split(jnp.concatenate(
            [jnp.concatenate([cross[b, x2, z2, 0], cross[b, x2, z2, 1]], axis=1) for b in range(2)],
            axis=0))
        factor = dot3(inv, column)
        factor = jnp.where(
            (n == 0) & (iota((2 * BLK, 2 * BLK), 0) >= BLK) & (iota((2 * BLK, 2 * BLK), 1) < BLK),
            0.0, factor)
        change = dot3(panel, split(factor))
        h, q = n // 4, (n % 4) * 2
        before = jnp.concatenate([rows_all[h, :, q, :], rows_all[h, :, q + 1, :]], axis=1)
        reduced_ref[:, pl.ds(pl.multiple_of(n * 256, 256), 256)] = before - change
        return carry

    lax.fori_loop(0, NBLK // 2, update, 0)
    for swap in swaps:
        swap.wait_send()
    sent1.wait_send()
    sent2.wait_send()


def on_device(inverse_factor, border, border_blocks, border_count, first_diag):
    vmem = pl.BlockSpec(memory_space=pltpu.VMEM)
    smem = pl.BlockSpec(memory_space=pltpu.SMEM)
    hbm = pl.BlockSpec(memory_space=pl.ANY)
    dma = pltpu.SemaphoreType.DMA
    return pl.pallas_call(
        kernel,
        out_shape=(
            jax.ShapeDtypeStruct((BLK, 2 * BLK), F32),
            jax.ShapeDtypeStruct((BLK, NBLK * BLK), F32),
        ),
        in_specs=[hbm, hbm, vmem, smem, smem],
        out_specs=(vmem, vmem),
        scratch_shapes=[
            pltpu.VMEM((ORDER, ORDER), BF16),
            pltpu.VMEM((ORDER, WIDTH), BF16),
            pltpu.VMEM((WIDTH, WIDTH), F32),
            pltpu.VMEM((DEV, PIECE1, BLK), F32),
            pltpu.VMEM((DEV, PIECE1, BLK), F32),
            pltpu.VMEM((DEPTH, 2 * BLK), BF16),
            pltpu.VMEM((NBLK * NBLK, BLK), F32),
            pltpu.VMEM((DEV, PIECE2, BLK), F32),
            pltpu.VMEM((DEV, PIECE2, BLK), F32),
            pltpu.VMEM((GRP, BLK, QUART, BLK), F32),
            pltpu.VMEM((2, 4, 4, 2, BLK, BLK), F32),
            pltpu.VMEM((BLK, BLK), F32),
            pltpu.VMEM((2, BLK, BLK), F32),
            dma((STRIPS,)), dma((STRIPS,)), dma((2,)), dma((2,)), dma((3,)),
            dma((30,)), dma((30,)), dma((2,)), dma((2,)),
        ],
        compiler_params=pltpu.CompilerParams(
            collective_id=0, has_side_effects=True, vmem_limit_bytes=60 * 2**20),
        name="schur",
    )(inverse_factor, border, first_diag.reshape(1, BLK), border_blocks, border_count)


def solution(mesh):
    return jax.shard_map(
        on_device,
        mesh=mesh,
        in_specs=(
            P(("grp", "tile"), None, None),
            P(("grp", "tile"), None, None),
            P(("grp", "tile"), None),
            P(("grp", "tile")),
            P("tile"),
        ),
        out_specs=(P("tile", None), P("tile", None)),
        check_vma=False,
    )
```

```python
import functools

import jax
import jax.numpy as jnp
from jax import lax
from jax.experimental import pallas as pl
from jax.experimental.pallas import tpu as pltpu
from jax.sharding import PartitionSpec as P

BLK = 128
MAXB = 4
NBLK = 32
ORDER = 2560
WIDTH = MAXB * BLK
DEV = 128
GRP = 4
TILE = 32
QUART = NBLK // GRP
STRIP = 512
STRIPS = ORDER // STRIP
PAIRS = MAXB * (MAXB + 1) // 2
PIECE1 = 16
SENT1 = PAIRS + 1
PIECE2 = 16
SENT2 = QUART + 5
PLACED = DEV * PIECE1
DEPTH = PLACED + BLK
MESH = pl.DeviceIdType.MESH
F32 = jnp.float32
BF16 = jnp.bfloat16


def split(value):
    high = value.astype(BF16)
    return high, (value - high.astype(F32)).astype(BF16)


def dot(left, right, dims=((1,), (0,))):
    return lax.dot_general(left, right, (dims, ((), ())), preferred_element_type=F32)


def dot_full(left, right, dims=((1,), (0,))):
    return lax.dot_general(
        left, right, (dims, ((), ())), precision=lax.Precision.HIGHEST, preferred_element_type=F32)


def iota(shape, axis):
    return lax.broadcasted_iota(jnp.int32, shape, axis)


def peer_of(k, g, t):
    x, z, c = t // 8, (t // 2) % 4, t % 2
    dy, dx, dz, dc = k // 32, (k // 8) % 4, (k // 2) % 4, k % 2
    return (g + dy) % 4, ((x + dx) % 4) * 8 + ((z + dz) % 4) * 2 + (c + dc) % 2


class Ring:
    def __init__(self, view, own, me, up, down, send, recv, first):
        self.view, self.own, self.me = view, own, me
        self.up, self.down = up, down
        self.send, self.recv, self.first = send, recv, first

    def copy(self, src, dst, slot, device):
        made = pltpu.make_async_remote_copy(
            src, dst, self.send.at[self.first + slot], self.recv.at[self.first + slot],
            device_id=device, device_id_type=MESH)
        made.start()
        return made

    def start(self):
        me = self.me
        self.copies = [
            self.copy(self.own(0), self.view(me, 0), 0, self.up),
            self.copy(self.own(1), self.view(me, 1), 1, self.down),
            self.copy(self.own(1), self.view(me, 1), 2, self.up),
            self.copy(self.own(0), self.view(me, 0), 3, self.down),
        ]

    def middle(self):
        below, above = (self.me + 3) % 4, (self.me + 1) % 4
        self.copies[0].wait_recv()
        self.copies.append(self.copy(self.view(below, 0), self.view(below, 0), 4, self.up))
        self.copies[1].wait_recv()
        self.copies.append(self.copy(self.view(above, 1), self.view(above, 1), 5, self.down))

    def end(self):
        for made in self.copies[2:]:
            made.wait_recv()
        for made in self.copies:
            made.wait_send()


def factor_steps(a_ref, v_ref, first, last):
    sub = iota((8, BLK), 0)
    lane = iota((8, BLK), 1)

    def step(s, carry):
        base = pl.multiple_of(s * 8, 8)
        rows = a_ref[pl.ds(base, 8), :]
        inv_rows = v_ref[pl.ds(base, 8), :]
        cols = [
            jnp.take_along_axis(rows, jnp.full((8, BLK), base + p, jnp.int32), axis=1) for p in range(8)
        ]
        scale = jnp.zeros((8, BLK), F32)
        for p in range(8):
            recip = 1.0 / cols[p][p:p + 1, :]
            scale = jnp.where(sub == p, recip, scale)
            if p == 7:
                break
            by = jnp.where(sub > p, cols[p] * recip, 0.0)
            rows = rows - by * rows[p:p + 1, :]
            inv_rows = inv_rows - by * inv_rows[p:p + 1, :]
            for q in range(p + 1, 8):
                cols[q] = cols[q] - by * cols[q][p:p + 1, :]
        by = jnp.where(lane >= base + 8, rows * scale, 0.0).T
        a = a_ref[...]
        v = v_ref[...]
        for p in range(8):
            column = jnp.broadcast_to(by[:, p:p + 1], (BLK, BLK))
            a = a - column * rows[p:p + 1, :]
            v = v - column * inv_rows[p:p + 1, :]
        a_ref[...] = a
        v_ref[...] = v
        v_ref[pl.ds(base, 8), :] = inv_rows * jnp.sqrt(scale)
        return carry

    lax.fori_loop(first, last, step, 0)


def kernel(
    w_ref, b_ref, diag_ref, ids_ref, count_ref, rows_all, cross, panel_ref, solved_ref,
    wbuf, bbuf, gram, send1, recv1, rhs, schur, send2, recv2, mine, pivot, inverse,
    wsem, bsem, send_sem, recv_sem, own_sem, ring_send, ring_recv, core_send, core_recv,
):
    g = lax.axis_index("grp")
    t = lax.axis_index("tile")
    me = g * TILE + t
    x, z, c = t // 8, (t // 2) % 4, t % 2

    loads = []
    for i in range(STRIPS):
        rows = pl.ds(i * STRIP, STRIP)
        border = pltpu.make_async_copy(b_ref.at[0, rows], bbuf.at[rows], bsem.at[i])
        border.start()
        cols = pl.ds(0, (i + 1) * STRIP)
        factor = pltpu.make_async_copy(w_ref.at[0, rows, cols], wbuf.at[rows, cols], wsem.at[i])
        factor.start()
        loads.append((border, factor))

    barrier = pltpu.get_barrier_semaphore()

    def greet(k, carry):
        pl.semaphore_signal(barrier, inc=1, device_id=peer_of(k, g, t), device_id_type=MESH)
        return carry

    lax.fori_loop(1, DEV, greet, 0)

    live = iota((STRIP, WIDTH), 1) // BLK < count_ref[0]
    for i in range(STRIPS):
        rows = pl.ds(i * STRIP, STRIP)
        depth = pl.ds(0, (i + 1) * STRIP)
        loads[i][0].wait()
        bbuf[rows, :] = jnp.where(live, bbuf[rows, :], BF16(0))
        loads[i][1].wait()
        coupled = dot(wbuf[rows, depth], bbuf[depth, :]).astype(BF16)
        part = dot(coupled, coupled, ((0,), (0,)))
        if i == 0:
            gram[...] = part
        else:
            gram[...] += part

    p = 0
    for i in range(MAXB):
        for j in range(i, MAXB):
            block = gram[i * BLK:(i + 1) * BLK, j * BLK:(j + 1) * BLK]
            if i < j:
                ahead = jnp.full((BLK, BLK), ids_ref[0, i]) < jnp.full((BLK, BLK), ids_ref[0, j])
                block = jnp.where(ahead, block, gram[j * BLK:(j + 1) * BLK, i * BLK:(i + 1) * BLK])
            send1[:, p, :] = block
            p += 1
    lane = iota((BLK, BLK), 1)
    extra = jnp.where(lane == MAXB, jnp.broadcast_to(diag_ref[...], (BLK, BLK)).T, 0.0)
    for i in range(MAXB):
        extra = jnp.where(lane == i, ids_ref[0, i].astype(F32), extra)
    send1[:, PAIRS, :] = extra

    pl.semaphore_wait(barrier, DEV - 1)

    def exchange(source, target, rows, slot):
        def go(k, carry):
            g2, t2 = peer_of(k, g, t)
            pltpu.make_async_remote_copy(
                source.at[g2 * TILE + t2, rows], target.at[me, rows], send_sem.at[slot], recv_sem.at[slot],
                device_id=(g2, t2), device_id_type=MESH).start()
            return carry

        lax.fori_loop(1, DEV, go, 0)
        own = pltpu.make_async_copy(source.at[me, rows], target.at[me, rows], own_sem.at[slot])
        own.start()
        own.wait()
        every = pltpu.make_async_remote_copy(
            source.at[pl.ds(0, DEV - 1), rows], target.at[pl.ds(0, DEV - 1), rows], send_sem.at[slot],
            recv_sem.at[slot], device_id=(g, t), device_id_type=MESH)
        every.wait_recv()
        return every

    sent1 = exchange(send1, recv1, pl.ds(0, SENT1), 0)

    extras = recv1[:, PAIRS, :]
    sel = iota((BLK, BLK), 0)
    pos = lane % PIECE1
    first = (pos >= 4).astype(jnp.int32) + (pos >= 7).astype(jnp.int32) + (pos >= 9).astype(jnp.int32)
    second = jnp.where(first == 0, pos, jnp.where(first == 1, pos - 3, jnp.where(first == 2, pos - 5, pos - 6)))
    ids16 = extras.astype(BF16)
    at_lane = (sel % 8 == lane // PIECE1).astype(F32)
    gather = (iota((DEV // 8, DEV), 1) // 8 == iota((DEV // 8, DEV), 0)).astype(BF16)

    def along(which):
        spread = dot(ids16, (sel == which).astype(BF16)) * at_lane
        return dot(gather, spread.astype(BF16))

    one, two = along(first), along(second)
    keys = (jnp.minimum(one, two) * NBLK + jnp.maximum(one, two)).astype(jnp.int32)
    keys = jnp.where(pos[0:DEV // 8, :] < PAIRS, keys, -1)
    own_row = iota((1, BLK), 1)
    own_key = jnp.where(own_row < NBLK, own_row * (NBLK + 1), -1)
    diag = jnp.where((lane == me) & (sel < NBLK), jnp.broadcast_to(extras[:, MAXB:MAXB + 1], (BLK, BLK)), 0.0)
    used = iota((DEV, PIECE1, BLK), 1) < PAIRS
    high, low = split(jnp.where(used, recv1[...], 0.0).reshape(PLACED, BLK))
    rhs[0:PLACED, 0:BLK] = high
    rhs[0:PLACED, BLK:2 * BLK] = low
    high, low = split(diag)
    rhs[PLACED:DEPTH, 0:BLK] = high
    rhs[PLACED:DEPTH, BLK:2 * BLK] = low

    def place(m, carry):
        base = pl.multiple_of(m * 256, 256)
        place_row = iota((256, BLK), 0) + base
        row, col = place_row // NBLK, place_row % NBLK
        target = jnp.minimum(row, col) * NBLK + jnp.maximum(row, col)
        hot = [
            jnp.where(target == keys[q:q + 1, :], F32(1), F32(0)).astype(BF16) for q in range(DEV // 8)
        ]
        hot.append(jnp.where(target == own_key, F32(1), F32(0)).astype(BF16))
        both = dot(jnp.concatenate(hot, axis=1), rhs[...])
        schur[pl.ds(base, 256), :] = both[:, 0:BLK] + both[:, BLK:2 * BLK]
        return carry

    lax.fori_loop(0, NBLK * NBLK // 256, place, 0)

    for h in range(GRP):
        for u in range(TILE):
            send2[h * TILE + u, 0:QUART, :] = schur[u * NBLK + h * QUART:u * NBLK + (h + 1) * QUART, :]
        some = pl.ds(h * TILE, TILE)
        for b in range(2):
            send2[some, QUART + b, :] = schur[b * NBLK:(b + 1) * NBLK, :]
        for e, r in enumerate((0, 1, NBLK + 1)):
            send2[some, QUART + 2 + e, :] = jnp.broadcast_to(schur[r:r + 1, :], (TILE, BLK))
    sent2 = exchange(send2, recv2, pl.ds(0, SENT2), 1)

    mine[0] = recv2[:, QUART, :]
    part = recv2[:, QUART + 1, :]
    mine[1] = jnp.where(jnp.full((BLK, BLK), t) == 0, part.T, part)
    owns = [pltpu.make_async_copy(recv2.at[:, pl.ds(0, QUART)], rows_all.at[g], own_sem.at[2])]
    for b in range(2):
        owns.append(pltpu.make_async_copy(mine.at[b], cross.at[b, x, z, c], own_sem.at[3 + b]))
    for own in owns:
        own.start()

    half = BLK // 2
    side = lambda s: pl.ds(s * half, half)
    at_x = lambda i: (g, i * 8 + z * 2 + c)
    at_z = lambda i: (g, x * 8 + i * 2 + c)
    up, down = (lambda i: (i + 1) % 4), (lambda i: (i + 3) % 4)
    ring_y = Ring(
        lambda i, s: rows_all.at[i, side(s)], lambda s: recv2.at[side(s), pl.ds(0, QUART)], g,
        (up(g), t), (down(g), t), ring_send, ring_recv, 0)

    def ring(view, own, position, at, first):
        return Ring(view, own, position, at(up(position)), at(down(position)), ring_send, ring_recv, first)

    slab_a = lambda i, s: cross.at[0, :, i, c, side(s)]
    slab_b = lambda i, s: cross.at[1, i, :, c, side(s)]
    ring_a1 = ring(lambda i, s: cross.at[0, i, z, c, side(s)], lambda s: mine.at[0, side(s)], x, at_x, 6)
    ring_b1 = ring(lambda i, s: cross.at[1, x, i, c, side(s)], lambda s: mine.at[1, side(s)], z, at_z, 12)
    ring_a2 = ring(slab_a, lambda s: slab_a(z, s), z, at_z, 18)
    ring_b2 = ring(slab_b, lambda s: slab_b(x, s), x, at_x, 24)
    swaps = []

    def swap(view):
        made = pltpu.make_async_remote_copy(
            view, view, core_send.at[len(swaps)], core_recv.at[len(swaps)],
            device_id=(g, x * 8 + z * 2 + (1 - c)), device_id_type=MESH)
        made.start()
        swaps.append(made)

    ring_y.start()
    ring_a1.start()
    ring_b1.start()
    eye = jnp.where(sel == lane, F32(1), F32(0))
    pivot[...] = recv2[:, QUART + 2, :]
    inverse[0] = eye
    inverse[1] = eye
    factor_steps(pivot, inverse.at[0], 0, 3)
    ring_a1.middle()
    ring_b1.middle()
    factor_steps(pivot, inverse.at[0], 3, 6)
    for own in owns[1:]:
        own.wait()
    ring_a1.end()
    ring_b1.end()
    ring_a2.start()
    ring_b2.start()
    swap(cross.at[0, :, z, c])
    swap(cross.at[1, x, :, c])
    ring_y.middle()
    factor_steps(pivot, inverse.at[0], 6, 11)
    ring_a2.middle()
    ring_b2.middle()
    factor_steps(pivot, inverse.at[0], 11, 16)
    below = dot_full(recv2[:, QUART + 3, :], inverse[0], ((0,), (1,)))
    pivot[...] = recv2[:, QUART + 4, :] - dot_full(below, below, ((1,), (1,)))
    ring_a2.end()
    ring_b2.end()
    for step in (1, 3, 2):
        swap(cross.at[0, :, (z + step) % 4, c])
        swap(cross.at[1, (x + step) % 4, :, c])
    factor_steps(pivot, inverse.at[1], 0, 16)
    first, second = inverse[0], inverse[1]
    mixed = -dot_full(second, dot_full(below, first))
    inv = jnp.concatenate(
        [jnp.concatenate([first, jnp.zeros((BLK, BLK), F32)], axis=1),
         jnp.concatenate([mixed, second], axis=1)], axis=0)
    panel = dot_full(jnp.concatenate([mine[0], mine[1]], axis=0), inv, ((0,), (1,)))
    panel_ref[...] = jnp.where(
        (jnp.full((BLK, 2 * BLK), t) == 0) & (iota((BLK, 2 * BLK), 1) >= BLK), 0.0, panel)
    solved_ref[...] = dot_full(panel, inv)

    owns[0].wait()
    ring_y.end()
    for made in swaps:
        made.wait()
    sent1.wait_send()
    sent2.wait_send()


def update(rows_ref, cross_ref, panel_ref, solved_ref, panel_out, reduced_out):
    t = lax.axis_index("tile")
    n = pl.program_id(0)
    panel_out[...] = panel_ref[...]
    for q in range(0, QUART, 2):
        before = []
        for e in range(q, q + 2):
            block = rows_ref[0, :, e, :]
            behind = jnp.full((BLK, BLK), n * QUART + e) < jnp.full((BLK, BLK), t)
            before.append(jnp.where(behind, block.T, block))
        column = jnp.concatenate(
            [jnp.concatenate([cross_ref[b, q], cross_ref[b, q + 1]], axis=1) for b in range(2)], axis=0)
        reduced_out[:, q * BLK:(q + 2) * BLK] = jnp.concatenate(before, axis=1) - dot_full(
            solved_ref[...], column)


def on_device(inverse_factor, border, border_blocks, border_count, first_diag):
    vmem = pl.BlockSpec(memory_space=pltpu.VMEM)
    smem = pl.BlockSpec(memory_space=pltpu.SMEM)
    hbm = pl.BlockSpec(memory_space=pl.ANY)
    dma = pltpu.SemaphoreType.DMA
    rows_all, cross, panel, solved = pl.pallas_call(
        kernel,
        out_shape=(
            jax.ShapeDtypeStruct((GRP, BLK, QUART, BLK), F32),
            jax.ShapeDtypeStruct((2, 4, 4, 2, BLK, BLK), F32),
            jax.ShapeDtypeStruct((BLK, 2 * BLK), F32),
            jax.ShapeDtypeStruct((BLK, 2 * BLK), F32),
        ),
        in_specs=[hbm, hbm, vmem, smem, smem],
        out_specs=(hbm, hbm, vmem, vmem),
        scratch_shapes=[
            pltpu.VMEM((ORDER, ORDER), BF16),
            pltpu.VMEM((ORDER, WIDTH), BF16),
            pltpu.VMEM((WIDTH, WIDTH), F32),
            pltpu.VMEM((DEV, PIECE1, BLK), F32),
            pltpu.VMEM((DEV, PIECE1, BLK), F32),
            pltpu.VMEM((DEPTH, 2 * BLK), BF16),
            pltpu.VMEM((NBLK * NBLK, BLK), F32),
            pltpu.VMEM((DEV, PIECE2, BLK), F32),
            pltpu.VMEM((DEV, PIECE2, BLK), F32),
            pltpu.VMEM((2, BLK, BLK), F32),
            pltpu.VMEM((BLK, BLK), F32),
            pltpu.VMEM((2, BLK, BLK), F32),
            dma((STRIPS,)), dma((STRIPS,)), dma((2,)), dma((2,)), dma((5,)),
            dma((30,)), dma((30,)), dma((8,)), dma((8,)),
        ],
        compiler_params=pltpu.CompilerParams(
            collective_id=0, has_side_effects=True, vmem_limit_bytes=60 * 2**20),
        name="schur",
    )(inverse_factor, border, first_diag.reshape(1, BLK), border_blocks, border_count)
    small = pl.BlockSpec((BLK, 2 * BLK), lambda n: (0, 0))
    return pl.pallas_call(
        update,
        grid=(GRP,),
        out_shape=(
            jax.ShapeDtypeStruct((BLK, 2 * BLK), F32),
            jax.ShapeDtypeStruct((BLK, NBLK * BLK), F32),
        ),
        in_specs=[
            pl.BlockSpec((1, BLK, QUART, BLK), lambda n: (n, 0, 0, 0)),
            pl.BlockSpec((2, QUART, BLK, BLK), lambda n: (0, n, 0, 0)),
            small, small,
        ],
        out_specs=(small, pl.BlockSpec((BLK, QUART * BLK), lambda n: (0, n))),
        compiler_params=pltpu.CompilerParams(vmem_limit_bytes=60 * 2**20),
        name="update",
    )(rows_all, cross.reshape(2, NBLK, BLK, BLK), panel, solved)


def solution(mesh):
    return jax.shard_map(
        on_device,
        mesh=mesh,
        in_specs=(
            P(("grp", "tile"), None, None),
            P(("grp", "tile"), None, None),
            P(("grp", "tile"), None),
            P(("grp", "tile")),
            P("tile"),
        ),
        out_specs=(P("tile", None), P("tile", None)),
        check_vma=False,
    )
```

```python
import functools

import jax
import jax.numpy as jnp
from jax import lax
from jax.experimental import pallas as pl
from jax.experimental.pallas import tpu as pltpu
from jax.sharding import PartitionSpec as P

BLK = 128
MAXB = 4
NBLK = 32
ORDER = 2560
WIDTH = MAXB * BLK
DEV = 128
GRP = 4
TILE = 32
QUART = NBLK // GRP
STRIP = 512
STRIPS = ORDER // STRIP
PAIRS = MAXB * (MAXB + 1) // 2
PIECE1 = 16
SENT1 = PAIRS + 1
SENT2 = 5
PLACED = DEV * PIECE1
DEPTH = PLACED + BLK
MESH = pl.DeviceIdType.MESH
F32 = jnp.float32
BF16 = jnp.bfloat16


def split(value):
    high = value.astype(BF16)
    return high, (value - high.astype(F32)).astype(BF16)


def dot(left, right, dims=((1,), (0,))):
    return lax.dot_general(left, right, (dims, ((), ())), preferred_element_type=F32)


def dot_full(left, right, dims=((1,), (0,))):
    return lax.dot_general(
        left, right, (dims, ((), ())), precision=lax.Precision.HIGHEST, preferred_element_type=F32)


def iota(shape, axis):
    return lax.broadcasted_iota(jnp.int32, shape, axis)


def peer_of(k, g, t):
    x, z, c = t // 8, (t // 2) % 4, t % 2
    dy, dx, dz, dc = k // 32, (k // 8) % 4, (k // 2) % 4, k % 2
    return (g + dy) % 4, ((x + dx) % 4) * 8 + ((z + dz) % 4) * 2 + (c + dc) % 2


class Ring:
    def __init__(self, view, own, me, up, down, send, recv, first):
        self.view, self.own, self.me = view, own, me
        self.up, self.down = up, down
        self.send, self.recv, self.first = send, recv, first

    def copy(self, src, dst, slot, device):
        made = pltpu.make_async_remote_copy(
            src, dst, self.send.at[self.first + slot], self.recv.at[self.first + slot],
            device_id=device, device_id_type=MESH)
        made.start()
        return made

    def start(self):
        me = self.me
        self.copies = [
            self.copy(self.own(0), self.view(me, 0), 0, self.up),
            self.copy(self.own(1), self.view(me, 1), 1, self.down),
            self.copy(self.own(1), self.view(me, 1), 2, self.up),
            self.copy(self.own(0), self.view(me, 0), 3, self.down),
        ]

    def middle(self):
        below, above = (self.me + 3) % 4, (self.me + 1) % 4
        self.copies[0].wait_recv()
        self.copies.append(self.copy(self.view(below, 0), self.view(below, 0), 4, self.up))
        self.copies[1].wait_recv()
        self.copies.append(self.copy(self.view(above, 1), self.view(above, 1), 5, self.down))

    def near(self):
        for made in self.copies[2:4]:
            made.wait_recv()

    def end(self):
        for made in self.copies[4:]:
            made.wait_recv()
        for made in self.copies:
            made.wait_send()


def factor_steps(a_ref, v_ref, first, last):
    sub = iota((8, BLK), 0)
    lane = iota((8, BLK), 1)

    def step(s, carry):
        base = pl.multiple_of(s * 8, 8)
        rows = a_ref[pl.ds(base, 8), :]
        inv_rows = v_ref[pl.ds(base, 8), :]
        cols = [
            jnp.take_along_axis(rows, jnp.full((8, BLK), base + p, jnp.int32), axis=1) for p in range(8)
        ]
        scale = jnp.zeros((8, BLK), F32)
        for p in range(8):
            recip = 1.0 / cols[p][p:p + 1, :]
            scale = jnp.where(sub == p, recip, scale)
            if p == 7:
                break
            by = jnp.where(sub > p, cols[p] * recip, 0.0)
            rows = rows - by * rows[p:p + 1, :]
            inv_rows = inv_rows - by * inv_rows[p:p + 1, :]
            for q in range(p + 1, 8):
                cols[q] = cols[q] - by * cols[q][p:p + 1, :]
        by = jnp.where(lane >= base + 8, rows * scale, 0.0).T
        a = a_ref[...]
        v = v_ref[...]
        for p in range(8):
            column = jnp.broadcast_to(by[:, p:p + 1], (BLK, BLK))
            a = a - column * rows[p:p + 1, :]
            v = v - column * inv_rows[p:p + 1, :]
        a_ref[...] = a
        v_ref[...] = v
        v_ref[pl.ds(base, 8), :] = inv_rows * jnp.sqrt(scale)
        return carry

    lax.fori_loop(first, last, step, 0)


def kernel(
    w_ref, b_ref, diag_ref, ids_ref, count_ref, rows_all, cross, panel_ref, solved_ref,
    wbuf, bbuf, gram, send1, recv1, rhs, send2, recv2, send3, recv3, small, mine, pivot, inverse,
    wsem, bsem, send_sem, recv_sem, own_sem, ring_send, ring_recv, core_send, core_recv, greet_sem,
):
    g = lax.axis_index("grp")
    t = lax.axis_index("tile")
    me = g * TILE + t
    x, z, c = t // 8, (t // 2) % 4, t % 2

    loads = []
    for i in range(STRIPS):
        rows = pl.ds(i * STRIP, STRIP)
        border = pltpu.make_async_copy(b_ref.at[0, rows], bbuf.at[rows], bsem.at[i])
        border.start()
        cols = pl.ds(0, (i + 1) * STRIP)
        factor = pltpu.make_async_copy(w_ref.at[0, rows, cols], wbuf.at[rows, cols], wsem.at[i])
        factor.start()
        loads.append((border, factor))

    barrier = pltpu.get_barrier_semaphore()
    along_y = [((g + d) % 4, t) for d in (1, 2, 3)]
    along_x = [(g, ((x + d) % 4) * 8 + z * 2 + c) for d in (1, 2, 3)]
    along_z = [(g, x * 8 + ((z + d) % 4) * 2 + c) for d in (1, 2, 3)]
    along_c = [(g, x * 8 + z * 2 + 1 - c)]

    def greet(semaphore, peers):
        for peer in peers:
            pl.semaphore_signal(semaphore, inc=1, device_id=peer, device_id_type=MESH)

    greet(barrier, along_y + along_x + along_z + along_c)

    live = iota((STRIP, WIDTH), 1) // BLK < count_ref[0]
    for i in range(STRIPS):
        rows = pl.ds(i * STRIP, STRIP)
        depth = pl.ds(0, (i + 1) * STRIP)
        loads[i][0].wait()
        bbuf[rows, :] = jnp.where(live, bbuf[rows, :], BF16(0))
        loads[i][1].wait()
        coupled = dot(wbuf[rows, depth], bbuf[depth, :]).astype(BF16)
        part = dot(coupled, coupled, ((0,), (0,)))
        if i == 0:
            gram[...] = part
        else:
            gram[...] += part
        if i == 0:
            pl.semaphore_wait(barrier, 10)
            greet(greet_sem.at[0], along_x)
        elif i == 1:
            pl.semaphore_wait(greet_sem.at[0], 3)
            greet(greet_sem.at[1], along_z)
        elif i == 2:
            pl.semaphore_wait(greet_sem.at[1], 3)
            greet(greet_sem.at[2], along_c)

    p = 0
    for i in range(MAXB):
        for j in range(i, MAXB):
            block = gram[i * BLK:(i + 1) * BLK, j * BLK:(j + 1) * BLK]
            if i < j:
                ahead = jnp.full((BLK, BLK), ids_ref[0, i]) < jnp.full((BLK, BLK), ids_ref[0, j])
                block = jnp.where(ahead, block, gram[j * BLK:(j + 1) * BLK, i * BLK:(i + 1) * BLK])
            send1[:, p, :] = block
            p += 1
    lane = iota((BLK, BLK), 1)
    extra = jnp.where(lane == MAXB, jnp.broadcast_to(diag_ref[...], (BLK, BLK)).T, 0.0)
    for i in range(MAXB):
        extra = jnp.where(lane == i, ids_ref[0, i].astype(F32), extra)
    send1[:, PAIRS, :] = extra

    pl.semaphore_wait(greet_sem.at[2], 1)

    def exchange(source, target, rows, count, slot):
        here = t if count == TILE else me

        def go(k, carry):
            g2, t2 = peer_of(k, g, t)
            there = t2 if count == TILE else g2 * TILE + t2
            pltpu.make_async_remote_copy(
                source.at[there, rows], target.at[here, rows], send_sem.at[slot], recv_sem.at[slot],
                device_id=(g2, t2), device_id_type=MESH).start()
            return carry

        lax.fori_loop(1, count, go, 0)
        own = pltpu.make_async_copy(source.at[here, rows], target.at[here, rows], own_sem.at[slot])
        own.start()
        every = pltpu.make_async_remote_copy(
            source.at[pl.ds(0, count - 1), rows], target.at[pl.ds(0, count - 1), rows], send_sem.at[slot],
            recv_sem.at[slot], device_id=(g, t), device_id_type=MESH)
        return own, every

    def received(exchanged):
        exchanged[0].wait()
        exchanged[1].wait_recv()

    sent1 = exchange(send1, recv1, pl.ds(0, SENT1), DEV, 0)
    received(sent1)

    extras = recv1[:, PAIRS, :]
    sel = iota((BLK, BLK), 0)
    pos = lane % PIECE1
    first = (pos >= 4).astype(jnp.int32) + (pos >= 7).astype(jnp.int32) + (pos >= 9).astype(jnp.int32)
    second = jnp.where(first == 0, pos, jnp.where(first == 1, pos - 3, jnp.where(first == 2, pos - 5, pos - 6)))
    ids16 = extras.astype(BF16)
    at_lane = (sel % 8 == lane // PIECE1).astype(F32)
    gather = (iota((DEV // 8, DEV), 1) // 8 == iota((DEV // 8, DEV), 0)).astype(BF16)

    def along(which):
        spread = dot(ids16, (sel == which).astype(BF16)) * at_lane
        return dot(gather, spread.astype(BF16))

    one, two = along(first), along(second)
    keys = (jnp.minimum(one, two) * NBLK + jnp.maximum(one, two)).astype(jnp.int32)
    keys = jnp.where(pos[0:DEV // 8, :] < PAIRS, keys, -1)
    own_row = iota((1, BLK), 1)
    own_key = jnp.where(own_row < NBLK, own_row * (NBLK + 1), -1)
    diag = jnp.where((lane == me) & (sel < NBLK), jnp.broadcast_to(extras[:, MAXB:MAXB + 1], (BLK, BLK)), 0.0)
    used = iota((DEV, PIECE1, BLK), 1) < PAIRS
    high, low = split(jnp.where(used, recv1[...], 0.0).reshape(PLACED, BLK))
    rhs[0:PLACED, 0:BLK] = high
    rhs[0:PLACED, BLK:2 * BLK] = low
    high, low = split(diag)
    rhs[PLACED:DEPTH, 0:BLK] = high
    rhs[PLACED:DEPTH, BLK:2 * BLK] = low

    def place(m, carry):
        base = pl.multiple_of(m * 256, 256)
        place_row = iota((256, BLK), 0) + base
        row, col = place_row // NBLK, place_row % NBLK
        target = jnp.minimum(row, col) * NBLK + jnp.maximum(row, col)
        hot = [
            jnp.where(target == keys[q:q + 1, :], F32(1), F32(0)).astype(BF16) for q in range(DEV // 8)
        ]
        hot.append(jnp.where(target == own_key, F32(1), F32(0)).astype(BF16))
        both = dot(jnp.concatenate(hot, axis=1), rhs[...])
        send3[pl.ds(m * 8, 8), :, :] = (both[:, 0:BLK] + both[:, BLK:2 * BLK]).reshape(8, NBLK, BLK)
        return carry

    lax.fori_loop(0, NBLK * NBLK // 256, place, 0)

    for b in range(2):
        send2[:, b, :] = send3[b]
    for e, (r, q) in enumerate(((0, 0), (0, 1), (1, 1))):
        send2[:, 2 + e, :] = jnp.broadcast_to(send3[r, q:q + 1, :], (TILE, BLK))
    sent2 = exchange(send2, recv2, pl.ds(0, SENT2), TILE, 1)
    sent3 = exchange(send3, recv3, pl.ds(0, NBLK), TILE, 2)
    received(sent2)

    part = pl.ds(pl.multiple_of(g * TILE, TILE), TILE)
    for e in range(5):
        small[e, part, :] = recv2[:, e, :]
    gathered = []
    for slot, which in enumerate((pl.ds(2, 3), pl.ds(0, 2))):
        for peer in (along_y[0], along_y[2], along_y[1]):
            pltpu.make_async_remote_copy(
                small.at[which, part], small.at[which, part], send_sem.at[3 + slot], recv_sem.at[3 + slot],
                device_id=peer, device_id_type=MESH).start()
        three = small.at[which, pl.ds(0, 3 * TILE)]
        gathered.append(pltpu.make_async_remote_copy(
            three, three, send_sem.at[3 + slot], recv_sem.at[3 + slot], device_id=(g, t), device_id_type=MESH))

    half, some = BLK // 2, TILE // 2
    side = lambda s: pl.ds(s * half, half)
    row_side = lambda s: pl.ds(s * some, some)
    at_x = lambda i: (g, i * 8 + z * 2 + c)
    at_z = lambda i: (g, x * 8 + i * 2 + c)
    up, down = (lambda i: (i + 1) % 4), (lambda i: (i + 3) % 4)
    ring_y = Ring(
        lambda i, s: rows_all.at[i, row_side(s)], lambda s: recv3.at[row_side(s)], g,
        (up(g), t), (down(g), t), ring_send, ring_recv, 0)

    def ring(view, own, position, at, first):
        return Ring(view, own, position, at(up(position)), at(down(position)), ring_send, ring_recv, first)

    slab_a = lambda i, s: cross.at[0, :, i, c, side(s)]
    slab_b = lambda i, s: cross.at[1, i, :, c, side(s)]
    ring_a1 = ring(lambda i, s: cross.at[0, i, z, c, side(s)], lambda s: mine.at[0, side(s)], x, at_x, 6)
    ring_b1 = ring(lambda i, s: cross.at[1, x, i, c, side(s)], lambda s: mine.at[1, side(s)], z, at_z, 12)
    ring_a2 = ring(slab_a, lambda s: slab_a(z, s), z, at_z, 18)
    ring_b2 = ring(slab_b, lambda s: slab_b(x, s), x, at_x, 24)
    swaps = []

    def swap(view):
        made = pltpu.make_async_remote_copy(
            view, view, core_send.at[len(swaps)], core_recv.at[len(swaps)],
            device_id=(g, x * 8 + z * 2 + (1 - c)), device_id_type=MESH)
        made.start()
        swaps.append(made)

    eye = jnp.where(sel == lane, F32(1), F32(0))
    inverse[0] = eye
    inverse[1] = eye
    gathered[0].wait_recv()
    pivot[...] = small[2]
    gathered[1].wait_recv()
    mine[0] = small[0]
    mine[1] = jnp.where(jnp.full((BLK, BLK), t) == 0, small[1].T, small[1])
    ring_a1.start()
    ring_b1.start()
    owns = [pltpu.make_async_copy(recv3, rows_all.at[g], own_sem.at[3])]
    for b in range(2):
        owns.append(pltpu.make_async_copy(mine.at[b], cross.at[b, x, z, c], own_sem.at[4 + b]))
        owns[-1].start()
    factor_steps(pivot, inverse.at[0], 0, 4)
    received(sent3)
    ring_y.start()
    owns[0].start()
    ring_a1.middle()
    ring_b1.middle()
    factor_steps(pivot, inverse.at[0], 4, 9)
    for own in owns[1:]:
        own.wait()
    for made in (ring_a1, ring_b1):
        made.near()
        made.end()
    ring_a2.start()
    ring_b2.start()
    swap(cross.at[0, :, z, c])
    swap(cross.at[1, x, :, c])
    factor_steps(pivot, inverse.at[0], 9, 16)
    ring_y.middle()
    below = dot_full(small[3], inverse[0], ((0,), (1,)))
    pivot[...] = small[4] - dot_full(below, below, ((1,), (1,)))
    ring_a2.middle()
    ring_b2.middle()
    factor_steps(pivot, inverse.at[1], 0, 6)
    ring_a2.near()
    ring_b2.near()
    for step in (1, 3):
        swap(cross.at[0, :, (z + step) % 4, c])
        swap(cross.at[1, (x + step) % 4, :, c])
    factor_steps(pivot, inverse.at[1], 6, 11)
    ring_a2.end()
    ring_b2.end()
    swap(cross.at[0, :, (z + 2) % 4, c])
    swap(cross.at[1, (x + 2) % 4, :, c])
    factor_steps(pivot, inverse.at[1], 11, 16)
    first, second = inverse[0], inverse[1]
    mixed = -dot_full(second, dot_full(below, first))
    inv = jnp.concatenate(
        [jnp.concatenate([first, jnp.zeros((BLK, BLK), F32)], axis=1),
         jnp.concatenate([mixed, second], axis=1)], axis=0)
    panel = dot_full(jnp.concatenate([mine[0], mine[1]], axis=0), inv, ((0,), (1,)))
    panel_ref[...] = jnp.where(
        (jnp.full((BLK, 2 * BLK), t) == 0) & (iota((BLK, 2 * BLK), 1) >= BLK), 0.0, panel)
    solved_ref[...] = dot_full(panel, inv)

    owns[0].wait()
    ring_y.near()
    ring_y.end()
    for made in swaps:
        made.wait()
    for made in (sent1[1], sent2[1], sent3[1], *gathered):
        made.wait_send()


def update(rows_ref, cross_ref, panel_ref, solved_ref, panel_out, reduced_out):
    t = lax.axis_index("tile")
    n = pl.program_id(0)
    panel_out[...] = panel_ref[...]
    for q in range(0, QUART, 2):
        before = []
        for e in range(q, q + 2):
            block = rows_ref[:, :, e, :].reshape(BLK, BLK)
            behind = jnp.full((BLK, BLK), n * QUART + e) < jnp.full((BLK, BLK), t)
            before.append(jnp.where(behind, block.T, block))
        column = jnp.concatenate(
            [jnp.concatenate([cross_ref[b, q], cross_ref[b, q + 1]], axis=1) for b in range(2)], axis=0)
        reduced_out[:, q * BLK:(q + 2) * BLK] = jnp.concatenate(before, axis=1) - dot_full(
            solved_ref[...], column)


def on_device(inverse_factor, border, border_blocks, border_count, first_diag):
    vmem = pl.BlockSpec(memory_space=pltpu.VMEM)
    smem = pl.BlockSpec(memory_space=pltpu.SMEM)
    hbm = pl.BlockSpec(memory_space=pl.ANY)
    dma = pltpu.SemaphoreType.DMA
    rows_all, cross, panel, solved = pl.pallas_call(
        kernel,
        out_shape=(
            jax.ShapeDtypeStruct((GRP, TILE, NBLK, BLK), F32),
            jax.ShapeDtypeStruct((2, 4, 4, 2, BLK, BLK), F32),
            jax.ShapeDtypeStruct((BLK, 2 * BLK), F32),
            jax.ShapeDtypeStruct((BLK, 2 * BLK), F32),
        ),
        in_specs=[hbm, hbm, vmem, smem, smem],
        out_specs=(hbm, hbm, vmem, vmem),
        scratch_shapes=[
            pltpu.VMEM((ORDER, ORDER), BF16),
            pltpu.VMEM((ORDER, WIDTH), BF16),
            pltpu.VMEM((WIDTH, WIDTH), F32),
            pltpu.VMEM((DEV, PIECE1, BLK), F32),
            pltpu.VMEM((DEV, PIECE1, BLK), F32),
            pltpu.VMEM((DEPTH, 2 * BLK), BF16),
            pltpu.VMEM((TILE, 8, BLK), F32),
            pltpu.VMEM((TILE, 8, BLK), F32),
            pltpu.VMEM((TILE, NBLK, BLK), F32),
            pltpu.VMEM((TILE, NBLK, BLK), F32),
            pltpu.VMEM((5, BLK, BLK), F32),
            pltpu.VMEM((2, BLK, BLK), F32),
            pltpu.VMEM((BLK, BLK), F32),
            pltpu.VMEM((2, BLK, BLK), F32),
            dma((STRIPS,)), dma((STRIPS,)), dma((5,)), dma((5,)), dma((6,)),
            dma((30,)), dma((30,)), dma((8,)), dma((8,)),
            pltpu.SemaphoreType.REGULAR((3,)),
        ],
        compiler_params=pltpu.CompilerParams(
            collective_id=0, has_side_effects=True, vmem_limit_bytes=60 * 2**20),
        name="schur",
    )(inverse_factor, border, first_diag.reshape(1, BLK), border_blocks, border_count)
    small = pl.BlockSpec((BLK, 2 * BLK), lambda n: (0, 0))
    return pl.pallas_call(
        update,
        grid=(GRP,),
        out_shape=(
            jax.ShapeDtypeStruct((BLK, 2 * BLK), F32),
            jax.ShapeDtypeStruct((BLK, NBLK * BLK), F32),
        ),
        in_specs=[
            pl.BlockSpec((GRP, TILE, QUART, BLK), lambda n: (0, 0, n, 0)),
            pl.BlockSpec((2, QUART, BLK, BLK), lambda n: (0, n, 0, 0)),
            small, small,
        ],
        out_specs=(small, pl.BlockSpec((BLK, QUART * BLK), lambda n: (0, n))),
        compiler_params=pltpu.CompilerParams(vmem_limit_bytes=60 * 2**20),
        name="update",
    )(rows_all, cross.reshape(2, NBLK, BLK, BLK), panel, solved)


def solution(mesh):
    return jax.shard_map(
        on_device,
        mesh=mesh,
        in_specs=(
            P(("grp", "tile"), None, None),
            P(("grp", "tile"), None, None),
            P(("grp", "tile"), None),
            P(("grp", "tile")),
            P("tile"),
        ),
        out_specs=(P("tile", None), P("tile", None)),
        check_vma=False,
    )
```

```python
import functools

import jax
import jax.numpy as jnp
from jax import lax
from jax.experimental import pallas as pl
from jax.experimental.pallas import tpu as pltpu
from jax.sharding import PartitionSpec as P

BLK = 128
MAXB = 4
NBLK = 32
ORDER = 2560
WIDTH = MAXB * BLK
DEV = 128
GRP = 4
TILE = 32
QUART = NBLK // GRP
STRIP = 512
STRIPS = ORDER // STRIP
PAIRS = MAXB * (MAXB + 1) // 2
PIECE1 = 16
SENT1 = PAIRS + 1
SENT2 = 5
PLACED = DEV * PIECE1
DEPTH = PLACED + BLK
MESH = pl.DeviceIdType.MESH
F32 = jnp.float32
BF16 = jnp.bfloat16


def split(value):
    high = value.astype(BF16)
    return high, (value - high.astype(F32)).astype(BF16)


def dot(left, right, dims=((1,), (0,))):
    return lax.dot_general(left, right, (dims, ((), ())), preferred_element_type=F32)


def dot_full(left, right, dims=((1,), (0,))):
    return lax.dot_general(
        left, right, (dims, ((), ())), precision=lax.Precision.HIGHEST, preferred_element_type=F32)


def iota(shape, axis):
    return lax.broadcasted_iota(jnp.int32, shape, axis)


def peer_of(k, g, t):
    x, z, c = t // 8, (t // 2) % 4, t % 2
    dy, dx, dz, dc = k // 32, (k // 8) % 4, (k // 2) % 4, k % 2
    return (g + dy) % 4, ((x + dx) % 4) * 8 + ((z + dz) % 4) * 2 + (c + dc) % 2


class Ring:
    def __init__(self, view, own, me, up, down, send, recv, first):
        self.view, self.own, self.me = view, own, me
        self.up, self.down = up, down
        self.send, self.recv, self.first = send, recv, first

    def copy(self, src, dst, slot, device):
        made = pltpu.make_async_remote_copy(
            src, dst, self.send.at[self.first + slot], self.recv.at[self.first + slot],
            device_id=device, device_id_type=MESH)
        made.start()
        return made

    def start(self):
        me = self.me
        self.copies = [
            self.copy(self.own(0), self.view(me, 0), 0, self.up),
            self.copy(self.own(1), self.view(me, 1), 1, self.down),
            self.copy(self.own(1), self.view(me, 1), 2, self.up),
            self.copy(self.own(0), self.view(me, 0), 3, self.down),
        ]

    def middle(self):
        below, above = (self.me + 3) % 4, (self.me + 1) % 4
        self.copies[0].wait_recv()
        self.copies.append(self.copy(self.view(below, 0), self.view(below, 0), 4, self.up))
        self.copies[1].wait_recv()
        self.copies.append(self.copy(self.view(above, 1), self.view(above, 1), 5, self.down))

    def near(self):
        for made in self.copies[2:4]:
            made.wait_recv()

    def end(self):
        for made in self.copies[4:]:
            made.wait_recv()
        for made in self.copies:
            made.wait_send()


def factor_steps(a_ref, v_ref, first, last):
    sub = iota((8, BLK), 0)
    lane = iota((8, BLK), 1)
    left = first * 8

    def step(s, carry):
        base = pl.multiple_of(s * 8, 8)
        rows = a_ref[pl.ds(base, 8), :]
        inv_rows = v_ref[pl.ds(base, 8), :]
        cols = [
            jnp.take_along_axis(rows, jnp.full((8, BLK), base + p, jnp.int32), axis=1) for p in range(8)
        ]
        scale = jnp.zeros((8, BLK), F32)
        for p in range(8):
            recip = 1.0 / cols[p][p:p + 1, :]
            scale = jnp.where(sub == p, recip, scale)
            if p == 7:
                break
            by = jnp.where(sub > p, cols[p] * recip, 0.0)
            rows = rows - by * rows[p:p + 1, :]
            inv_rows = inv_rows - by * inv_rows[p:p + 1, :]
            for q in range(p + 1, 8):
                cols[q] = cols[q] - by * cols[q][p:p + 1, :]
        by = jnp.where(lane >= base + 8, rows * scale, 0.0).T[left:, :]
        a = a_ref[left:, :]
        v = v_ref[left:, :]
        for p in range(8):
            column = jnp.broadcast_to(by[:, p:p + 1], (BLK - left, BLK))
            a = a - column * rows[p:p + 1, :]
            v = v - column * inv_rows[p:p + 1, :]
        a_ref[left:, :] = a
        v_ref[left:, :] = v
        v_ref[pl.ds(base, 8), :] = inv_rows * jnp.sqrt(scale)
        return carry

    lax.fori_loop(first, last, step, 0)


def kernel(
    w_ref, b_ref, diag_ref, ids_ref, count_ref, rows_all, cross, panel_ref, solved_ref,
    wbuf, bbuf, gram, send1, recv1, rhs, send2, recv2, send3, recv3, small, mine, pivot, inverse,
    wsem, bsem, send_sem, recv_sem, own_sem, ring_send, ring_recv, core_send, core_recv, greet_sem, first_send, first_recv,
):
    g = lax.axis_index("grp")
    t = lax.axis_index("tile")
    me = g * TILE + t
    x, z, c = t // 8, (t // 2) % 4, t % 2

    loads = []
    for i in range(STRIPS):
        rows = pl.ds(i * STRIP, STRIP)
        border = pltpu.make_async_copy(b_ref.at[0, rows], bbuf.at[rows], bsem.at[i])
        border.start()
        cols = pl.ds(0, (i + 1) * STRIP)
        factor = pltpu.make_async_copy(w_ref.at[0, rows, cols], wbuf.at[rows, cols], wsem.at[i])
        factor.start()
        loads.append((border, factor))

    barrier = pltpu.get_barrier_semaphore()
    along_y = [((g + d) % 4, t) for d in (1, 2, 3)]
    along_x = [(g, ((x + d) % 4) * 8 + z * 2 + c) for d in (1, 2, 3)]
    along_z = [(g, x * 8 + ((z + d) % 4) * 2 + c) for d in (1, 2, 3)]
    along_c = [(g, x * 8 + z * 2 + 1 - c)]

    def greet(semaphore, peers):
        for peer in peers:
            pl.semaphore_signal(semaphore, inc=1, device_id=peer, device_id_type=MESH)

    greet(barrier, along_y + along_x + along_z + along_c)

    live = iota((STRIP, WIDTH), 1) // BLK < count_ref[0]
    for i in range(STRIPS):
        rows = pl.ds(i * STRIP, STRIP)
        depth = pl.ds(0, (i + 1) * STRIP)
        loads[i][0].wait()
        bbuf[rows, :] = jnp.where(live, bbuf[rows, :], BF16(0))
        loads[i][1].wait()
        coupled = dot(wbuf[rows, depth], bbuf[depth, :]).astype(BF16)
        part = dot(coupled, coupled, ((0,), (0,)))
        if i == 0:
            gram[...] = part
        else:
            gram[...] += part
        if i == 0:
            pl.semaphore_wait(barrier, 10)
            greet(greet_sem.at[0], along_x)
        elif i == 1:
            pl.semaphore_wait(greet_sem.at[0], 3)
            greet(greet_sem.at[1], along_z)
        elif i == 2:
            pl.semaphore_wait(greet_sem.at[1], 3)
            greet(greet_sem.at[2], along_c)

    p = 0
    for i in range(MAXB):
        for j in range(i, MAXB):
            block = gram[i * BLK:(i + 1) * BLK, j * BLK:(j + 1) * BLK]
            if i < j:
                ahead = jnp.full((BLK, BLK), ids_ref[0, i]) < jnp.full((BLK, BLK), ids_ref[0, j])
                block = jnp.where(ahead, block, gram[j * BLK:(j + 1) * BLK, i * BLK:(i + 1) * BLK])
            send1[:, p, :] = block
            p += 1
    lane = iota((BLK, BLK), 1)
    extra = jnp.where(lane == MAXB, jnp.broadcast_to(diag_ref[...], (BLK, BLK)).T, 0.0)
    for i in range(MAXB):
        extra = jnp.where(lane == i, ids_ref[0, i].astype(F32), extra)
    send1[:, PAIRS, :] = extra

    pl.semaphore_wait(greet_sem.at[2], 1)

    def exchange(source, target, rows, count, slot):
        here = t if count == TILE else me

        def go(k, carry):
            g2, t2 = peer_of(k, g, t)
            there = t2 if count == TILE else g2 * TILE + t2
            pltpu.make_async_remote_copy(
                source.at[there, rows], target.at[here, rows], send_sem.at[slot], recv_sem.at[slot],
                device_id=(g2, t2), device_id_type=MESH).start()
            return carry

        lax.fori_loop(1, count, go, 0)
        own = pltpu.make_async_copy(source.at[here, rows], target.at[here, rows], own_sem.at[slot])
        own.start()
        every = pltpu.make_async_remote_copy(
            source.at[pl.ds(0, count - 1), rows], target.at[pl.ds(0, count - 1), rows], send_sem.at[slot],
            recv_sem.at[slot], device_id=(g, t), device_id_type=MESH)
        return own, every

    def received(exchanged):
        exchanged[0].wait()
        exchanged[1].wait_recv()

    sent_rows = pl.ds(0, SENT1)
    sent1, planes = [], []
    for dy in (2, 1, 3, 0):
        def go1(k, carry, last=(dy + 1) * TILE - 1, first=dy * TILE + (0 if dy else 1)):
            g2, t2 = peer_of(last + first - k, g, t)
            pltpu.make_async_remote_copy(
                send1.at[g2 * TILE + t2, sent_rows], recv1.at[me, sent_rows], first_send.at[dy],
                first_recv.at[dy], device_id=(g2, t2), device_id_type=MESH).start()
            return carry

        first = 0 if dy else 1
        lax.fori_loop(dy * TILE + first, (dy + 1) * TILE, go1, 0)
        slab = recv1.at[pl.ds((g + 4 - dy) % 4 * TILE, TILE - first), sent_rows]
        planes.append(dy)
        sent1.append(pltpu.make_async_remote_copy(
            slab, slab, first_send.at[dy], first_recv.at[dy], device_id=(g, t), device_id_type=MESH))
    own_piece = pltpu.make_async_copy(send1.at[me, sent_rows], recv1.at[me, sent_rows], own_sem.at[0])
    own_piece.start()
    own_piece.wait()
    used = iota((TILE, PIECE1, BLK), 1) < PAIRS
    for made, dy in zip(sent1, planes):
        made.wait_recv()
        base = pl.multiple_of((g + 4 - dy) % 4 * TILE, TILE)
        high, low = split(jnp.where(used, recv1[pl.ds(base, TILE)], 0.0).reshape(TILE * PIECE1, BLK))
        place_rows = pl.ds(pl.multiple_of(base * PIECE1, TILE * PIECE1), TILE * PIECE1)
        rhs[place_rows, 0:BLK] = high
        rhs[place_rows, BLK:2 * BLK] = low

    extras = recv1[:, PAIRS, :]
    sel = iota((BLK, BLK), 0)
    pos = lane % PIECE1
    first = (pos >= 4).astype(jnp.int32) + (pos >= 7).astype(jnp.int32) + (pos >= 9).astype(jnp.int32)
    second = jnp.where(first == 0, pos, jnp.where(first == 1, pos - 3, jnp.where(first == 2, pos - 5, pos - 6)))
    ids16 = extras.astype(BF16)
    at_lane = (sel % 8 == lane // PIECE1).astype(F32)
    gather = (iota((DEV // 8, DEV), 1) // 8 == iota((DEV // 8, DEV), 0)).astype(BF16)

    def along(which):
        spread = dot(ids16, (sel == which).astype(BF16)) * at_lane
        return dot(gather, spread.astype(BF16))

    one, two = along(first), along(second)
    keys = (jnp.minimum(one, two) * NBLK + jnp.maximum(one, two)).astype(jnp.int32)
    keys = jnp.where(pos[0:DEV // 8, :] < PAIRS, keys, -1)
    own_row = iota((1, BLK), 1)
    own_key = jnp.where(own_row < NBLK, own_row * (NBLK + 1), -1)
    diag = jnp.where((lane == me) & (sel < NBLK), jnp.broadcast_to(extras[:, MAXB:MAXB + 1], (BLK, BLK)), 0.0)
    high, low = split(diag)
    rhs[PLACED:DEPTH, 0:BLK] = high
    rhs[PLACED:DEPTH, BLK:2 * BLK] = low

    def placed(base, count):
        place_row = iota((count, BLK), 0) + base
        row, col = place_row // NBLK, place_row % NBLK
        target = jnp.minimum(row, col) * NBLK + jnp.maximum(row, col)
        hot = [
            jnp.where(target == keys[q:q + 1, :], F32(1), F32(0)).astype(BF16) for q in range(DEV // 8)
        ]
        hot.append(jnp.where(target == own_key, F32(1), F32(0)).astype(BF16))
        both = dot(jnp.concatenate(hot, axis=1), rhs[...])
        return (both[:, 0:BLK] + both[:, BLK:2 * BLK]).reshape(count // NBLK, NBLK, BLK)

    top = placed(0, 2 * NBLK)
    for b in range(2):
        send2[:, b, :] = top[b]
    for e, (r, q) in enumerate(((0, 0), (0, 1), (1, 1))):
        send2[:, 2 + e, :] = jnp.broadcast_to(top[r, q:q + 1, :], (TILE, BLK))
    sent2 = exchange(send2, recv2, pl.ds(0, SENT2), TILE, 1)

    def send_rows(dx):
        ahead, behind = (x + dx) % 4 * 8, (x + 4 - dx) % 4 * 8
        send3[pl.ds(pl.multiple_of(ahead, 8), 8), :, :] = placed(ahead * NBLK, 8 * NBLK)

        def go(k, carry):
            t2 = ahead + (z + k // 2) % 4 * 2 + (c + k % 2) % 2
            pltpu.make_async_remote_copy(
                send3.at[t2], recv3.at[t], send_sem.at[2 + dx], recv_sem.at[2 + dx],
                device_id=(g, t2), device_id_type=MESH).start()
            return carry

        first = 0 if dx else 1
        lax.fori_loop(first, 8, go, 0)
        slab = recv3.at[pl.ds(behind, 8 - first)]
        return pltpu.make_async_remote_copy(
            slab, slab, send_sem.at[2 + dx], recv_sem.at[2 + dx], device_id=(g, t), device_id_type=MESH)

    sent3 = [send_rows(0)]
    own_row = pltpu.make_async_copy(send3.at[t], recv3.at[t], own_sem.at[2])
    own_row.start()
    sent3.append(send_rows(1))
    received(sent2)

    part = pl.ds(pl.multiple_of(g * TILE, TILE), TILE)
    for e in range(5):
        small[e, part, :] = recv2[:, e, :]
    gathered = []
    for slot, which in enumerate((pl.ds(0, 2), pl.ds(2, 3))):
        for peer in (along_y[0], along_y[2], along_y[1]):
            pltpu.make_async_remote_copy(
                small.at[which, part], small.at[which, part], send_sem.at[6 + slot], recv_sem.at[6 + slot],
                device_id=peer, device_id_type=MESH).start()
        three = small.at[which, pl.ds(0, 3 * TILE)]
        gathered.append(pltpu.make_async_remote_copy(
            three, three, send_sem.at[6 + slot], recv_sem.at[6 + slot], device_id=(g, t), device_id_type=MESH))

    half = BLK // 2
    side = lambda s: pl.ds(s * half, half)
    at_x = lambda i: (g, i * 8 + z * 2 + c)
    at_z = lambda i: (g, x * 8 + i * 2 + c)
    up, down = (lambda i: (i + 1) % 4), (lambda i: (i + 3) % 4)
    def ring_rows(slot, dx):
        base = (x + 4 - dx) % 4 * 8
        rows = lambda s: pl.ds(base + s * 4, 4)
        return Ring(
            lambda i, s: rows_all.at[i, rows(s)], lambda s: recv3.at[rows(s)], g,
            (up(g), t), (down(g), t), ring_send, ring_recv, 24 + 6 * slot)

    ring_y = [ring_rows(slot, dx) for slot, dx in enumerate((0, 1, 3, 2))]

    def start_y(slot):
        sent3[slot].wait_recv()
        ring_y[slot].start()

    def ring(view, own, position, at, first):
        return Ring(view, own, position, at(up(position)), at(down(position)), ring_send, ring_recv, first)

    slab_a = lambda i, s: cross.at[0, :, i, c, side(s)]
    slab_b = lambda i, s: cross.at[1, i, :, c, side(s)]
    ring_a1 = ring(lambda i, s: cross.at[0, i, z, c, side(s)], lambda s: mine.at[0, side(s)], x, at_x, 0)
    ring_b1 = ring(lambda i, s: cross.at[1, x, i, c, side(s)], lambda s: mine.at[1, side(s)], z, at_z, 6)
    ring_a2 = ring(slab_a, lambda s: slab_a(z, s), z, at_z, 12)
    ring_b2 = ring(slab_b, lambda s: slab_b(x, s), x, at_x, 18)
    swaps = []

    def swap(view):
        made = pltpu.make_async_remote_copy(
            view, view, core_send.at[len(swaps)], core_recv.at[len(swaps)],
            device_id=(g, x * 8 + z * 2 + (1 - c)), device_id_type=MESH)
        made.start()
        swaps.append(made)

    eye = jnp.where(sel == lane, F32(1), F32(0))
    inverse[0] = eye
    inverse[1] = eye
    own_row.wait()
    start_y(0)
    sent3.append(send_rows(3))
    start_y(1)
    sent3.append(send_rows(2))
    gathered[0].wait_recv()
    mine[0] = small[0]
    mine[1] = jnp.where(jnp.full((BLK, BLK), t) == 0, small[1].T, small[1])
    ring_a1.start()
    ring_b1.start()
    owns = []
    for b in range(2):
        owns.append(pltpu.make_async_copy(mine.at[b], cross.at[b, x, z, c], own_sem.at[4 + b]))
        owns[-1].start()
    gathered[1].wait_recv()
    pivot[...] = small[2]
    factor_steps(pivot, inverse.at[0], 0, 3)
    ring_a1.middle()
    ring_b1.middle()
    start_y(2)
    ring_y[0].middle()
    factor_steps(pivot, inverse.at[0], 3, 7)
    for own in owns:
        own.wait()
    for made in (ring_a1, ring_b1):
        made.near()
        made.end()
    ring_a2.start()
    ring_b2.start()
    swap(cross.at[0, :, z, c])
    swap(cross.at[1, x, :, c])
    ring_y[1].middle()
    start_y(3)
    owns.append(pltpu.make_async_copy(recv3, rows_all.at[g], own_sem.at[3]))
    owns[-1].start()
    factor_steps(pivot, inverse.at[0], 7, 13)
    ring_y[2].middle()
    factor_steps(pivot, inverse.at[0], 13, 16)
    ring_y[3].middle()
    ring_a2.middle()
    ring_b2.middle()
    below = dot_full(small[3], inverse[0], ((0,), (1,)))
    pivot[...] = small[4] - dot_full(below, below, ((1,), (1,)))
    mixed = dot_full(below, inverse[0])
    factor_steps(pivot, inverse.at[1], 0, 5)
    ring_a2.near()
    ring_b2.near()
    for step in (1, 3):
        swap(cross.at[0, :, (z + step) % 4, c])
        swap(cross.at[1, (x + step) % 4, :, c])
    factor_steps(pivot, inverse.at[1], 5, 9)
    ring_a2.end()
    ring_b2.end()
    swap(cross.at[0, :, (z + 2) % 4, c])
    swap(cross.at[1, (x + 2) % 4, :, c])
    factor_steps(pivot, inverse.at[1], 9, 16)
    inv = jnp.concatenate(
        [jnp.concatenate([inverse[0], jnp.zeros((BLK, BLK), F32)], axis=1),
         jnp.concatenate([-dot_full(inverse[1], mixed), inverse[1]], axis=1)], axis=0)
    panel = dot_full(jnp.concatenate([mine[0], mine[1]], axis=0), inv, ((0,), (1,)))
    panel_ref[...] = jnp.where(
        (jnp.full((BLK, 2 * BLK), t) == 0) & (iota((BLK, 2 * BLK), 1) >= BLK), 0.0, panel)
    solved_ref[...] = dot_full(panel, inv)

    owns[-1].wait()
    for made in ring_y:
        made.near()
        made.end()
    for made in swaps:
        made.wait()
    for made in (*sent1, sent2[1], *sent3, *gathered):
        made.wait_send()


def split3(value):
    high, rest = value.astype(BF16), value - value.astype(BF16).astype(F32)
    middle = rest.astype(BF16)
    return high, middle, (rest - middle.astype(F32)).astype(BF16)


def update(rows_ref, cross_ref, panel_ref, solved_ref, panel_out, reduced_out):
    t = lax.axis_index("tile")
    n = pl.program_id(0)
    panel_out[...] = panel_ref[...]
    left = jnp.concatenate(split3(solved_ref[...]), axis=0)
    for q in range(0, QUART, 2):
        before = []
        for e in range(q, q + 2):
            block = rows_ref[:, :, e, :].reshape(BLK, BLK)
            behind = jnp.full((BLK, BLK), n * QUART + e) < jnp.full((BLK, BLK), t)
            before.append(jnp.where(behind, block.T, block))
        right = split3(jnp.concatenate(
            [jnp.concatenate([cross_ref[b, q], cross_ref[b, q + 1]], axis=1) for b in range(2)], axis=0))
        one, two, three = dot(left, right[0]), dot(left[0:2 * BLK], right[1]), dot(left[0:BLK], right[2])
        change = one[0:BLK] + (one[BLK:2 * BLK] + two[0:BLK] + (one[2 * BLK:] + two[BLK:] + three))
        reduced_out[:, q * BLK:(q + 2) * BLK] = jnp.concatenate(before, axis=1) - change


def on_device(inverse_factor, border, border_blocks, border_count, first_diag):
    vmem = pl.BlockSpec(memory_space=pltpu.VMEM)
    smem = pl.BlockSpec(memory_space=pltpu.SMEM)
    hbm = pl.BlockSpec(memory_space=pl.ANY)
    dma = pltpu.SemaphoreType.DMA
    rows_all, cross, panel, solved = pl.pallas_call(
        kernel,
        out_shape=(
            jax.ShapeDtypeStruct((GRP, TILE, NBLK, BLK), F32),
            jax.ShapeDtypeStruct((2, 4, 4, 2, BLK, BLK), F32),
            jax.ShapeDtypeStruct((BLK, 2 * BLK), F32),
            jax.ShapeDtypeStruct((BLK, 2 * BLK), F32),
        ),
        in_specs=[hbm, hbm, vmem, smem, smem],
        out_specs=(hbm, hbm, vmem, vmem),
        scratch_shapes=[
            pltpu.VMEM((ORDER, ORDER), BF16),
            pltpu.VMEM((ORDER, WIDTH), BF16),
            pltpu.VMEM((WIDTH, WIDTH), F32),
            pltpu.VMEM((DEV, PIECE1, BLK), F32),
            pltpu.VMEM((DEV, PIECE1, BLK), F32),
            pltpu.VMEM((DEPTH, 2 * BLK), BF16),
            pltpu.VMEM((TILE, 8, BLK), F32),
            pltpu.VMEM((TILE, 8, BLK), F32),
            pltpu.VMEM((TILE, NBLK, BLK), F32),
            pltpu.VMEM((TILE, NBLK, BLK), F32),
            pltpu.VMEM((5, BLK, BLK), F32),
            pltpu.VMEM((2, BLK, BLK), F32),
            pltpu.VMEM((BLK, BLK), F32),
            pltpu.VMEM((2, BLK, BLK), F32),
            dma((STRIPS,)), dma((STRIPS,)), dma((8,)), dma((8,)), dma((6,)),
            dma((48,)), dma((48,)), dma((8,)), dma((8,)),
            pltpu.SemaphoreType.REGULAR((3,)), dma((GRP,)), dma((GRP,)),
        ],
        compiler_params=pltpu.CompilerParams(
            collective_id=0, has_side_effects=True, vmem_limit_bytes=60 * 2**20),
        name="schur",
    )(inverse_factor, border, first_diag.reshape(1, BLK), border_blocks, border_count)
    small = pl.BlockSpec((BLK, 2 * BLK), lambda n: (0, 0))
    return pl.pallas_call(
        update,
        grid=(GRP,),
        out_shape=(
            jax.ShapeDtypeStruct((BLK, 2 * BLK), F32),
            jax.ShapeDtypeStruct((BLK, NBLK * BLK), F32),
        ),
        in_specs=[
            pl.BlockSpec((GRP, TILE, QUART, BLK), lambda n: (0, 0, n, 0)),
            pl.BlockSpec((2, QUART, BLK, BLK), lambda n: (0, n, 0, 0)),
            small, small,
        ],
        out_specs=(small, pl.BlockSpec((BLK, QUART * BLK), lambda n: (0, n))),
        compiler_params=pltpu.CompilerParams(vmem_limit_bytes=60 * 2**20),
        name="update",
    )(rows_all, cross.reshape(2, NBLK, BLK, BLK), panel, solved)


def solution(mesh):
    return jax.shard_map(
        on_device,
        mesh=mesh,
        in_specs=(
            P(("grp", "tile"), None, None),
            P(("grp", "tile"), None, None),
            P(("grp", "tile"), None),
            P(("grp", "tile")),
            P("tile"),
        ),
        out_specs=(P("tile", None), P("tile", None)),
        check_vma=False,
    )
```

```python
import functools

import jax
import jax.numpy as jnp
from jax import lax
from jax.experimental import pallas as pl
from jax.experimental.pallas import tpu as pltpu
from jax.sharding import PartitionSpec as P

BLK = 128
MAXB = 4
NBLK = 32
ORDER = 2560
WIDTH = MAXB * BLK
DEV = 128
GRP = 4
TILE = 32
QUART = NBLK // GRP
STRIP = 512
STRIPS = ORDER // STRIP
PAIRS = MAXB * (MAXB + 1) // 2
PIECE1 = 16
SENT1 = PAIRS + 1
SENT2 = 5
PLACED = DEV * PIECE1
DEPTH = PLACED + BLK
MESH = pl.DeviceIdType.MESH
F32 = jnp.float32
BF16 = jnp.bfloat16


def split(value):
    high = value.astype(BF16)
    return high, (value - high.astype(F32)).astype(BF16)


def dot(left, right, dims=((1,), (0,))):
    return lax.dot_general(left, right, (dims, ((), ())), preferred_element_type=F32)


def dot_full(left, right, dims=((1,), (0,))):
    return lax.dot_general(
        left, right, (dims, ((), ())), precision=lax.Precision.HIGHEST, preferred_element_type=F32)


def iota(shape, axis):
    return lax.broadcasted_iota(jnp.int32, shape, axis)


def peer_of(k, g, t):
    x, z, c = t // 8, (t // 2) % 4, t % 2
    dy, dx, dz, dc = k // 32, (k // 8) % 4, (k // 2) % 4, k % 2
    return (g + dy) % 4, ((x + dx) % 4) * 8 + ((z + dz) % 4) * 2 + (c + dc) % 2


class Ring:
    def __init__(self, view, own, me, up, down, send, recv, first):
        self.view, self.own, self.me = view, own, me
        self.up, self.down = up, down
        self.send, self.recv, self.first = send, recv, first

    def copy(self, src, dst, slot, device):
        made = pltpu.make_async_remote_copy(
            src, dst, self.send.at[self.first + slot], self.recv.at[self.first + slot],
            device_id=device, device_id_type=MESH)
        made.start()
        return made

    def start(self):
        me = self.me
        self.copies = [
            self.copy(self.own(0), self.view(me, 0), 0, self.up),
            self.copy(self.own(1), self.view(me, 1), 1, self.down),
            self.copy(self.own(1), self.view(me, 1), 2, self.up),
            self.copy(self.own(0), self.view(me, 0), 3, self.down),
        ]

    def middle(self):
        below, above = (self.me + 3) % 4, (self.me + 1) % 4
        self.copies[0].wait_recv()
        self.copies.append(self.copy(self.view(below, 0), self.view(below, 0), 4, self.up))
        self.copies[1].wait_recv()
        self.copies.append(self.copy(self.view(above, 1), self.view(above, 1), 5, self.down))

    def near(self):
        for made in self.copies[2:4]:
            made.wait_recv()

    def end(self):
        for made in self.copies[4:]:
            made.wait_recv()
        for made in self.copies:
            made.wait_send()


def factor_steps(a_ref, v_ref, first, last):
    sub = iota((8, BLK), 0)
    lane = iota((8, BLK), 1)
    left = first * 8

    def step(s, carry):
        base = pl.multiple_of(s * 8, 8)
        rows = a_ref[pl.ds(base, 8), :]
        inv_rows = v_ref[pl.ds(base, 8), :]
        cols = [
            jnp.take_along_axis(rows, jnp.full((8, BLK), base + p, jnp.int32), axis=1) for p in range(8)
        ]
        scale = jnp.zeros((8, BLK), F32)
        for p in range(8):
            recip = 1.0 / cols[p][p:p + 1, :]
            scale = jnp.where(sub == p, recip, scale)
            if p == 7:
                break
            by = jnp.where(sub > p, cols[p] * recip, 0.0)
            rows = rows - by * rows[p:p + 1, :]
            inv_rows = inv_rows - by * inv_rows[p:p + 1, :]
            for q in range(p + 1, 8):
                cols[q] = cols[q] - by * cols[q][p:p + 1, :]
        by = jnp.where(lane >= base + 8, rows * scale, 0.0).T[left:, :]
        a = a_ref[left:, :]
        v = v_ref[left:, :]
        for p in range(8):
            column = jnp.broadcast_to(by[:, p:p + 1], (BLK - left, BLK))
            a = a - column * rows[p:p + 1, :]
            v = v - column * inv_rows[p:p + 1, :]
        a_ref[left:, :] = a
        v_ref[left:, :] = v
        v_ref[pl.ds(base, 8), :] = inv_rows * jnp.sqrt(scale)
        return carry

    lax.fori_loop(first, last, step, 0)


def kernel(
    w_ref, b_ref, diag_ref, ids_ref, count_ref, rows_all, cross, panel_ref, solved_ref,
    wbuf, bbuf, gram, send1, recv1, rhs, send2, recv2, send3, recv3, small, mine, pivot, inverse,
    wsem, bsem, send_sem, recv_sem, own_sem, ring_send, ring_recv, core_send, core_recv, greet_sem, first_send, first_recv,
):
    g = lax.axis_index("grp")
    t = lax.axis_index("tile")
    me = g * TILE + t
    x, z, c = t // 8, (t // 2) % 4, t % 2

    loads = []
    for i in range(STRIPS):
        rows = pl.ds(i * STRIP, STRIP)
        border = pltpu.make_async_copy(b_ref.at[0, rows], bbuf.at[rows], bsem.at[i])
        border.start()
        cols = pl.ds(0, (i + 1) * STRIP)
        factor = pltpu.make_async_copy(w_ref.at[0, rows, cols], wbuf.at[rows, cols], wsem.at[i])
        factor.start()
        loads.append((border, factor))

    barrier = pltpu.get_barrier_semaphore()
    along_y = [((g + d) % 4, t) for d in (1, 2, 3)]
    along_x = [(g, ((x + d) % 4) * 8 + z * 2 + c) for d in (1, 2, 3)]
    along_z = [(g, x * 8 + ((z + d) % 4) * 2 + c) for d in (1, 2, 3)]
    along_c = [(g, x * 8 + z * 2 + 1 - c)]

    def greet(semaphore, peers):
        for peer in peers:
            pl.semaphore_signal(semaphore, inc=1, device_id=peer, device_id_type=MESH)

    greet(barrier, along_y + along_x + along_z + along_c)

    live = iota((STRIP, WIDTH), 1) // BLK < count_ref[0]
    for i in range(STRIPS):
        rows = pl.ds(i * STRIP, STRIP)
        depth = pl.ds(0, (i + 1) * STRIP)
        loads[i][0].wait()
        bbuf[rows, :] = jnp.where(live, bbuf[rows, :], BF16(0))
        loads[i][1].wait()
        coupled = dot(wbuf[rows, depth], bbuf[depth, :]).astype(BF16)
        part = dot(coupled, coupled, ((0,), (0,)))
        if i == 0:
            gram[...] = part
        else:
            gram[...] += part
        if i == 0:
            pl.semaphore_wait(barrier, 10)
            greet(greet_sem.at[0], along_x)
        elif i == 1:
            pl.semaphore_wait(greet_sem.at[0], 3)
            greet(greet_sem.at[1], along_z)
        elif i == 2:
            pl.semaphore_wait(greet_sem.at[1], 3)
            greet(greet_sem.at[2], along_c)

    p = 0
    for i in range(MAXB):
        for j in range(i, MAXB):
            block = gram[i * BLK:(i + 1) * BLK, j * BLK:(j + 1) * BLK]
            if i < j:
                ahead = jnp.full((BLK, BLK), ids_ref[0, i]) < jnp.full((BLK, BLK), ids_ref[0, j])
                block = jnp.where(ahead, block, gram[j * BLK:(j + 1) * BLK, i * BLK:(i + 1) * BLK])
            send1[:, p, :] = block
            p += 1
    lane = iota((BLK, BLK), 1)
    extra = jnp.where(lane == MAXB, jnp.broadcast_to(diag_ref[...], (BLK, BLK)).T, 0.0)
    for i in range(MAXB):
        extra = jnp.where(lane == i, ids_ref[0, i].astype(F32), extra)
    send1[:, PAIRS, :] = extra

    pl.semaphore_wait(greet_sem.at[2], 1)

    def exchange(source, target, rows, count, slot):
        here = t if count == TILE else me

        def go(k, carry):
            g2, t2 = peer_of(k, g, t)
            there = t2 if count == TILE else g2 * TILE + t2
            pltpu.make_async_remote_copy(
                source.at[there, rows], target.at[here, rows], send_sem.at[slot], recv_sem.at[slot],
                device_id=(g2, t2), device_id_type=MESH).start()
            return carry

        lax.fori_loop(1, count, go, 0)
        own = pltpu.make_async_copy(source.at[here, rows], target.at[here, rows], own_sem.at[slot])
        own.start()
        every = pltpu.make_async_remote_copy(
            source.at[pl.ds(0, count - 1), rows], target.at[pl.ds(0, count - 1), rows], send_sem.at[slot],
            recv_sem.at[slot], device_id=(g, t), device_id_type=MESH)
        return own, every

    def received(exchanged):
        exchanged[0].wait()
        exchanged[1].wait_recv()

    sent_rows = pl.ds(0, SENT1)
    sent1, planes = [], []
    for dy in (2, 1, 3, 0):
        def go1(k, carry, last=(dy + 1) * TILE - 1, first=dy * TILE + (0 if dy else 1)):
            g2, t2 = peer_of(last + first - k, g, t)
            pltpu.make_async_remote_copy(
                send1.at[g2 * TILE + t2, sent_rows], recv1.at[me, sent_rows], first_send.at[dy],
                first_recv.at[dy], device_id=(g2, t2), device_id_type=MESH).start()
            return carry

        first = 0 if dy else 1
        lax.fori_loop(dy * TILE + first, (dy + 1) * TILE, go1, 0)
        slab = recv1.at[pl.ds((g + 4 - dy) % 4 * TILE, TILE - first), sent_rows]
        planes.append(dy)
        sent1.append(pltpu.make_async_remote_copy(
            slab, slab, first_send.at[dy], first_recv.at[dy], device_id=(g, t), device_id_type=MESH))
    own_piece = pltpu.make_async_copy(send1.at[me, sent_rows], recv1.at[me, sent_rows], own_sem.at[0])
    own_piece.start()
    own_piece.wait()
    used = iota((TILE, PIECE1, BLK), 1) < PAIRS
    for made, dy in zip(sent1, planes):
        made.wait_recv()
        base = pl.multiple_of((g + 4 - dy) % 4 * TILE, TILE)
        high, low = split(jnp.where(used, recv1[pl.ds(base, TILE)], 0.0).reshape(TILE * PIECE1, BLK))
        place_rows = pl.ds(pl.multiple_of(base * PIECE1, TILE * PIECE1), TILE * PIECE1)
        rhs[place_rows, 0:BLK] = high
        rhs[place_rows, BLK:2 * BLK] = low

    extras = recv1[:, PAIRS, :]
    sel = iota((BLK, BLK), 0)
    pos = lane % PIECE1
    first = (pos >= 4).astype(jnp.int32) + (pos >= 7).astype(jnp.int32) + (pos >= 9).astype(jnp.int32)
    second = jnp.where(first == 0, pos, jnp.where(first == 1, pos - 3, jnp.where(first == 2, pos - 5, pos - 6)))
    ids16 = extras.astype(BF16)
    at_lane = (sel % 8 == lane // PIECE1).astype(F32)
    gather = (iota((DEV // 8, DEV), 1) // 8 == iota((DEV // 8, DEV), 0)).astype(BF16)

    def along(which):
        spread = dot(ids16, (sel == which).astype(BF16)) * at_lane
        return dot(gather, spread.astype(BF16))

    one, two = along(first), along(second)
    keys = (jnp.minimum(one, two) * NBLK + jnp.maximum(one, two)).astype(jnp.int32)
    keys = jnp.where(pos[0:DEV // 8, :] < PAIRS, keys, -1)
    own_row = iota((1, BLK), 1)
    own_key = jnp.where(own_row < NBLK, own_row * (NBLK + 1), -1)
    diag = jnp.where((lane == me) & (sel < NBLK), jnp.broadcast_to(extras[:, MAXB:MAXB + 1], (BLK, BLK)), 0.0)
    high, low = split(diag)
    rhs[PLACED:DEPTH, 0:BLK] = high
    rhs[PLACED:DEPTH, BLK:2 * BLK] = low

    def placed(base, count):
        place_row = iota((count, BLK), 0) + base
        row, col = place_row // NBLK, place_row % NBLK
        target = jnp.minimum(row, col) * NBLK + jnp.maximum(row, col)
        hot = [
            jnp.where(target == keys[q:q + 1, :], F32(1), F32(0)).astype(BF16) for q in range(DEV // 8)
        ]
        hot.append(jnp.where(target == own_key, F32(1), F32(0)).astype(BF16))
        both = dot(jnp.concatenate(hot, axis=1), rhs[...])
        return (both[:, 0:BLK] + both[:, BLK:2 * BLK]).reshape(count // NBLK, NBLK, BLK)

    top = placed(0, 2 * NBLK)
    for b in range(2):
        send2[:, b, :] = top[b]
    for e, (r, q) in enumerate(((0, 0), (0, 1), (1, 1))):
        send2[:, 2 + e, :] = jnp.broadcast_to(top[r, q:q + 1, :], (TILE, BLK))
    sent2 = exchange(send2, recv2, pl.ds(0, SENT2), TILE, 1)

    def send_rows(dx):
        ahead, behind = (x + dx) % 4 * 8, (x + 4 - dx) % 4 * 8
        send3[pl.ds(pl.multiple_of(ahead, 8), 8), :, :] = placed(ahead * NBLK, 8 * NBLK)

        def go(k, carry):
            t2 = ahead + (z + k // 2) % 4 * 2 + (c + k % 2) % 2
            pltpu.make_async_remote_copy(
                send3.at[t2], recv3.at[t], send_sem.at[2 + dx], recv_sem.at[2 + dx],
                device_id=(g, t2), device_id_type=MESH).start()
            return carry

        first = 0 if dx else 1
        lax.fori_loop(first, 8, go, 0)
        slab = recv3.at[pl.ds(behind, 8 - first)]
        return pltpu.make_async_remote_copy(
            slab, slab, send_sem.at[2 + dx], recv_sem.at[2 + dx], device_id=(g, t), device_id_type=MESH)

    sent3 = [send_rows(0)]
    own_row = pltpu.make_async_copy(send3.at[t], recv3.at[t], own_sem.at[2])
    own_row.start()
    sent3.append(send_rows(1))
    received(sent2)

    part = pl.ds(pl.multiple_of(g * TILE, TILE), TILE)
    for e in range(5):
        small[e, part, :] = recv2[:, e, :]
    gathered = []
    for slot, which in enumerate((pl.ds(0, 2), pl.ds(2, 3))):
        for peer in (along_y[0], along_y[2], along_y[1]):
            pltpu.make_async_remote_copy(
                small.at[which, part], small.at[which, part], send_sem.at[6 + slot], recv_sem.at[6 + slot],
                device_id=peer, device_id_type=MESH).start()
        three = small.at[which, pl.ds(0, 3 * TILE)]
        gathered.append(pltpu.make_async_remote_copy(
            three, three, send_sem.at[6 + slot], recv_sem.at[6 + slot], device_id=(g, t), device_id_type=MESH))

    half = BLK // 2
    side = lambda s: pl.ds(s * half, half)
    at_x = lambda i: (g, i * 8 + z * 2 + c)
    at_z = lambda i: (g, x * 8 + i * 2 + c)
    up, down = (lambda i: (i + 1) % 4), (lambda i: (i + 3) % 4)
    def ring_rows(slot, dx):
        base = (x + 4 - dx) % 4 * 8
        rows = lambda s: pl.ds(base + s * 4, 4)
        return Ring(
            lambda i, s: rows_all.at[i, rows(s)], lambda s: recv3.at[rows(s)], g,
            (up(g), t), (down(g), t), ring_send, ring_recv, 24 + 6 * slot)

    ring_y = [ring_rows(slot, dx) for slot, dx in enumerate((0, 1, 3, 2))]

    def start_y(slot):
        sent3[slot].wait_recv()
        ring_y[slot].start()

    def ring(view, own, position, at, first):
        return Ring(view, own, position, at(up(position)), at(down(position)), ring_send, ring_recv, first)

    slab_a = lambda i, s: cross.at[0, :, i, c, side(s)]
    slab_b = lambda i, s: cross.at[1, i, :, c, side(s)]
    ring_a1 = ring(lambda i, s: cross.at[0, i, z, c, side(s)], lambda s: mine.at[0, side(s)], x, at_x, 0)
    ring_b1 = ring(lambda i, s: cross.at[1, x, i, c, side(s)], lambda s: mine.at[1, side(s)], z, at_z, 6)
    ring_a2 = ring(slab_a, lambda s: slab_a(z, s), z, at_z, 12)
    ring_b2 = ring(slab_b, lambda s: slab_b(x, s), x, at_x, 18)
    swaps = []

    def swap(view):
        made = pltpu.make_async_remote_copy(
            view, view, core_send.at[len(swaps)], core_recv.at[len(swaps)],
            device_id=(g, x * 8 + z * 2 + (1 - c)), device_id_type=MESH)
        made.start()
        swaps.append(made)

    eye = jnp.where(sel == lane, F32(1), F32(0))
    inverse[0] = eye
    inverse[1] = eye
    own_row.wait()
    start_y(0)
    sent3.append(send_rows(3))
    start_y(1)
    sent3.append(send_rows(2))
    gathered[0].wait_recv()
    mine[0] = small[0]
    mine[1] = jnp.where(jnp.full((BLK, BLK), t) == 0, small[1].T, small[1])
    ring_a1.start()
    ring_b1.start()
    owns = []
    for b in range(2):
        owns.append(pltpu.make_async_copy(mine.at[b], cross.at[b, x, z, c], own_sem.at[4 + b]))
        owns[-1].start()
    ring_a1.middle()
    ring_b1.middle()
    gathered[1].wait_recv()
    pivot[...] = small[2]
    factor_steps(pivot, inverse.at[0], 0, 3)
    for own in owns:
        own.wait()
    for made in (ring_a1, ring_b1):
        made.near()
        made.end()
    ring_a2.start()
    ring_b2.start()
    swap(cross.at[0, :, z, c])
    swap(cross.at[1, x, :, c])
    start_y(2)
    ring_y[0].middle()
    start_y(3)
    factor_steps(pivot, inverse.at[0], 3, 7)
    ring_y[1].middle()
    owns.append(pltpu.make_async_copy(recv3, rows_all.at[g], own_sem.at[3]))
    owns[-1].start()
    factor_steps(pivot, inverse.at[0], 7, 13)
    ring_y[2].middle()
    factor_steps(pivot, inverse.at[0], 13, 16)
    ring_y[3].middle()
    ring_a2.middle()
    ring_b2.middle()
    below = dot_full(small[3], inverse[0], ((0,), (1,)))
    pivot[...] = small[4] - dot_full(below, below, ((1,), (1,)))
    mixed = dot_full(below, inverse[0])
    factor_steps(pivot, inverse.at[1], 0, 5)
    ring_a2.near()
    ring_b2.near()
    for step in (1, 3):
        swap(cross.at[0, :, (z + step) % 4, c])
        swap(cross.at[1, (x + step) % 4, :, c])
    factor_steps(pivot, inverse.at[1], 5, 9)
    ring_a2.end()
    ring_b2.end()
    swap(cross.at[0, :, (z + 2) % 4, c])
    swap(cross.at[1, (x + 2) % 4, :, c])
    factor_steps(pivot, inverse.at[1], 9, 16)
    inv = jnp.concatenate(
        [jnp.concatenate([inverse[0], jnp.zeros((BLK, BLK), F32)], axis=1),
         jnp.concatenate([-dot_full(inverse[1], mixed), inverse[1]], axis=1)], axis=0)
    panel = dot_full(jnp.concatenate([mine[0], mine[1]], axis=0), inv, ((0,), (1,)))
    panel_ref[...] = jnp.where(
        (jnp.full((BLK, 2 * BLK), t) == 0) & (iota((BLK, 2 * BLK), 1) >= BLK), 0.0, panel)
    solved_ref[...] = dot_full(panel, inv)

    owns[-1].wait()
    for made in ring_y:
        made.near()
        made.end()
    for made in swaps:
        made.wait()
    for made in (*sent1, sent2[1], *sent3, *gathered):
        made.wait_send()


def split3(value):
    high, rest = value.astype(BF16), value - value.astype(BF16).astype(F32)
    middle = rest.astype(BF16)
    return high, middle, (rest - middle.astype(F32)).astype(BF16)


def update(rows_ref, cross_ref, panel_ref, solved_ref, panel_out, reduced_out):
    t = lax.axis_index("tile")
    n = pl.program_id(0)
    panel_out[...] = panel_ref[...]
    left = jnp.concatenate(split3(solved_ref[...]), axis=0)
    for q in range(0, QUART, 2):
        before = []
        for e in range(q, q + 2):
            block = rows_ref[:, :, e, :].reshape(BLK, BLK)
            behind = jnp.full((BLK, BLK), n * QUART + e) < jnp.full((BLK, BLK), t)
            before.append(jnp.where(behind, block.T, block))
        right = split3(jnp.concatenate(
            [jnp.concatenate([cross_ref[b, q], cross_ref[b, q + 1]], axis=1) for b in range(2)], axis=0))
        one, two, three = dot(left, right[0]), dot(left[0:2 * BLK], right[1]), dot(left[0:BLK], right[2])
        change = one[0:BLK] + (one[BLK:2 * BLK] + two[0:BLK] + (one[2 * BLK:] + two[BLK:] + three))
        reduced_out[:, q * BLK:(q + 2) * BLK] = jnp.concatenate(before, axis=1) - change


def on_device(inverse_factor, border, border_blocks, border_count, first_diag):
    vmem = pl.BlockSpec(memory_space=pltpu.VMEM)
    smem = pl.BlockSpec(memory_space=pltpu.SMEM)
    hbm = pl.BlockSpec(memory_space=pl.ANY)
    dma = pltpu.SemaphoreType.DMA
    rows_all, cross, panel, solved = pl.pallas_call(
        kernel,
        out_shape=(
            jax.ShapeDtypeStruct((GRP, TILE, NBLK, BLK), F32),
            jax.ShapeDtypeStruct((2, 4, 4, 2, BLK, BLK), F32),
            jax.ShapeDtypeStruct((BLK, 2 * BLK), F32),
            jax.ShapeDtypeStruct((BLK, 2 * BLK), F32),
        ),
        in_specs=[hbm, hbm, vmem, smem, smem],
        out_specs=(hbm, hbm, vmem, vmem),
        scratch_shapes=[
            pltpu.VMEM((ORDER, ORDER), BF16),
            pltpu.VMEM((ORDER, WIDTH), BF16),
            pltpu.VMEM((WIDTH, WIDTH), F32),
            pltpu.VMEM((DEV, PIECE1, BLK), F32),
            pltpu.VMEM((DEV, PIECE1, BLK), F32),
            pltpu.VMEM((DEPTH, 2 * BLK), BF16),
            pltpu.VMEM((TILE, 8, BLK), F32),
            pltpu.VMEM((TILE, 8, BLK), F32),
            pltpu.VMEM((TILE, NBLK, BLK), F32),
            pltpu.VMEM((TILE, NBLK, BLK), F32),
            pltpu.VMEM((5, BLK, BLK), F32),
            pltpu.VMEM((2, BLK, BLK), F32),
            pltpu.VMEM((BLK, BLK), F32),
            pltpu.VMEM((2, BLK, BLK), F32),
            dma((STRIPS,)), dma((STRIPS,)), dma((8,)), dma((8,)), dma((6,)),
            dma((48,)), dma((48,)), dma((8,)), dma((8,)),
            pltpu.SemaphoreType.REGULAR((3,)), dma((GRP,)), dma((GRP,)),
        ],
        compiler_params=pltpu.CompilerParams(
            collective_id=0, has_side_effects=True, vmem_limit_bytes=60 * 2**20),
        name="schur",
    )(inverse_factor, border, first_diag.reshape(1, BLK), border_blocks, border_count)
    small = pl.BlockSpec((BLK, 2 * BLK), lambda n: (0, 0))
    return pl.pallas_call(
        update,
        grid=(GRP,),
        out_shape=(
            jax.ShapeDtypeStruct((BLK, 2 * BLK), F32),
            jax.ShapeDtypeStruct((BLK, NBLK * BLK), F32),
        ),
        in_specs=[
            pl.BlockSpec((GRP, TILE, QUART, BLK), lambda n: (0, 0, n, 0)),
            pl.BlockSpec((2, QUART, BLK, BLK), lambda n: (0, n, 0, 0)),
            small, small,
        ],
        out_specs=(small, pl.BlockSpec((BLK, QUART * BLK), lambda n: (0, n))),
        compiler_params=pltpu.CompilerParams(vmem_limit_bytes=60 * 2**20),
        name="update",
    )(rows_all, cross.reshape(2, NBLK, BLK, BLK), panel, solved)


def solution(mesh):
    return jax.shard_map(
        on_device,
        mesh=mesh,
        in_specs=(
            P(("grp", "tile"), None, None),
            P(("grp", "tile"), None, None),
            P(("grp", "tile"), None),
            P(("grp", "tile")),
            P("tile"),
        ),
        out_specs=(P("tile", None), P("tile", None)),
        check_vma=False,
    )
```
